512 devices in a mesh: ctx: 64 (over x, z_lo, core), tp: 8 (over z_hi, y).
Axes of the slice: x: 4, y: 4, z: 16 (z_hi: 2, z_lo: 8; z = z_hi * 8 + z_lo), core: 2. Of those that a mesh axis runs over, the one named last changes fastest.
Arguments:
- tokens: bfloat16 [8192, 8192], P('ctx', 'tp'), may hold values from -6 to 6
- in_weight: bfloat16 [3, 8192, 1024], P(None, 'ctx', 'tp'), may hold values from -0.0625 to 0.0625
- short_taps: float32 [3, 1024, 3], P(None, 'tp'), may hold values from -3 to 3
- residues: float32 [1024, 16], P('tp'), may hold values from -1.5 to 1.5
- rates: float32 [1024, 16], P('tp'), may hold values from 0.00012207031 to 0.03
- skip_gain: float32 [1024], P('tp'), may hold values from 0.5 to 1.5
Outputs:
- gated: float32 [1024, 8192], P('tp', 'ctx')
The draws below stay inside these ranges and needn't reach their ends.
All inputs are finite; a program needn't handle non-finite values.
Results may differ from the reference program's by a relative error of at most 0.0049.
Values may be sent and summed in bfloat16 or wider, within the bound.
No kernel may reach another device: no remote copies, remote signals or barrier semaphores. Data moves between devices by JAX's collectives and lax.ppermute only.
A program may use at most 64 MiB of HBM per device.

```python
import math
import jax
import jax.numpy as jnp
from jax import lax

D = 8192
C = 1024
MODES = 16
SEQ = 8192


def level_of(stream_key, shape, pieces, least, top_value):
    loudness, own = 1.0, jax.random.fold_in(stream_key, 6)
    for position, shards_of in pieces:
        steps = jnp.exp(jax.random.uniform(jax.random.fold_in(own, position), (shards_of,), jnp.float32, least / len(pieces), top_value / len(pieces)))
        loudness = loudness * jnp.repeat(steps, shape[position] // shards_of).reshape([-1 if axis == position else 1 for axis in range(len(shape))])
    return loudness


def noise(rng, dims, spread, most, shards=(), kind=jnp.bfloat16):
    level = level_of(rng, dims, shards, -0.22, 0.18) if shards else 1.0
    entries = jax.random.normal(rng, dims, jnp.float32) * spread * level
    return jnp.minimum(jnp.maximum(entries, -most), most).astype(kind)


def setup_inputs(seed: int = 0) -> dict:
    arg_keys = jax.random.split(jax.random.key(seed), 7)
    return {
        "tokens": noise(arg_keys[0], (SEQ, D), 1.0, 6.0, ((0, 64), (1, 8))),
        "in_weight": noise(arg_keys[1], (3, D, C), D ** -0.5, 0.0625, ((1, 64), (2, 8))),
        "short_taps": noise(arg_keys[2], (3, C, 3), 0.6, 3.0, ((1, 8),), jnp.float32),
        "residues": noise(arg_keys[3], (C, MODES), 0.25, 1.5, ((0, 8),), jnp.float32),
        "rates": jnp.clip(jnp.exp(math.log(0.03) - 5.5043554 * jax.random.uniform(arg_keys[4], (C, MODES), jnp.float32) ** level_of(arg_keys[4], (C, MODES), ((0, 8),), -0.2, 0.2)), 0.00012207031, 0.03),
        "skip_gain": jnp.clip(1.0 + 0.1 * jax.random.normal(arg_keys[5], (C,), jnp.float32), 0.5, 1.5),
    }


def block_conv(packed):
    driven, residues, rates = packed
    positions = jnp.arange(SEQ).astype(jnp.float32)
    amplitude = residues * jnp.sqrt(2.0 * rates)
    kernel = lax.optimization_barrier(jnp.sum(amplitude[:, :, None] * jnp.exp(-rates[:, :, None] * positions[None, None, :]), axis=1))
    length = 2 * SEQ
    product = jnp.fft.fft(driven, n=length, axis=1) * jnp.fft.fft(kernel, n=length, axis=1)
    return jnp.real(jnp.fft.ifft(product, axis=1))[:, :SEQ].astype(driven.dtype)

def reference(tokens, in_weight, short_taps, residues, rates, skip_gain):
    wide_tokens = tokens.astype(jnp.float32)
    proj = jnp.stack([jnp.dot(wide_tokens, in_weight[j].astype(jnp.float32), preferred_element_type=jnp.float32).T for j in range(3)])
    proj = proj.astype(jnp.bfloat16)
    wide = jnp.pad(proj.astype(jnp.float32), ((0, 0), (0, 0), (2, 0)))
    filtered = short_taps[:, :, 0:1] * wide[:, :, 2:] + short_taps[:, :, 1:2] * wide[:, :, 1:-1] + short_taps[:, :, 2:3] * wide[:, :, :-2]
    query = filtered[0]
    driven = filtered[1] * filtered[2]
    blocks = C // 64
    conv = lax.map(block_conv, (driven.reshape(blocks, 64, SEQ), residues.reshape(blocks, 64, MODES), rates.reshape(blocks, 64, MODES)))
    conv = conv.reshape(C, SEQ)
    return query * (conv + skip_gain[:, None] * driven)
```

```python
import jax
import jax.numpy as jnp
from jax import lax
from jax.experimental import pallas as pl
from jax.experimental.pallas import tpu as pltpu
from jax.sharding import PartitionSpec as P

F32 = jnp.float32
BF16 = jnp.bfloat16
HALO = 16
BLOCK = 128
MODES = 16
VMEM = pl.BlockSpec(memory_space=pltpu.VMEM)
SMEM = pl.BlockSpec(memory_space=pltpu.SMEM)
PARAMS = pltpu.CompilerParams(vmem_limit_bytes=48 * 1024 * 1024)


def flip(x, axis, mask):
    length = lax.axis_size(axis)
    return lax.ppermute(x, axis, [(i, i ^ mask) for i in range(length)])


def ahead(x, axis, by):
    length = lax.axis_size(axis)
    return lax.ppermute(x, axis, [(i, i + by) for i in range(length - by)])


def ordered(upper, own, other, axis):
    first = jnp.where(upper, other, own)
    second = jnp.where(upper, own, other)
    return jnp.concatenate([first, second], axis=axis)


def gather_tokens(tokens, core):
    split = tokens.reshape(BLOCK, 2, 2, 2, BLOCK)
    kept = lax.dynamic_index_in_dim(split, core, 3, keepdims=False)
    given = lax.dynamic_index_in_dim(split, 1 - core, 3, keepdims=False)
    kept = kept.reshape(BLOCK, 2, 256).transpose(1, 0, 2)
    given = given.reshape(BLOCK, 2, 256).transpose(1, 0, 2)
    other = flip(given, "ctx", 1)
    both = ordered(core == 1, kept, other, 1)
    halo = ahead(both[:, 2 * BLOCK - HALO :], "ctx", 2)
    rows = jnp.concatenate([halo, both], axis=1)
    pair = jnp.stack([rows, flip(rows, "tp", 4)])
    turns = [pair] + [flip(pair, "tp", m) for m in (1, 3, 2)]
    return jnp.stack([turns[0], turns[1], turns[3], turns[2]])


def gather_weights(piece, place):
    held = piece[None]
    held = jnp.concatenate([held, flip(held, "ctx", 8)], axis=0)
    held = jnp.concatenate([held, flip(held, "ctx", 4)], axis=0)
    held = ordered((place & 2) == 2, held, flip(held, "ctx", 2), 1)
    return [held] + [flip(held, "ctx", m << 4) for m in (1, 2, 3)]


def project_kernel(order, tokens, w0, w1, w2, w3, out):
    total = jnp.zeros(out.shape, F32)
    for i, w in enumerate((w0, w1, w2, w3)):
        for j in range(4):
            total += jnp.dot(tokens[order[4 * i + j]], w[j], preferred_element_type=F32)
    out[...] = total


def project(order, tokens, weights):
    rows, columns = tokens.shape[1], weights[0].shape[2]
    return pl.pallas_call(
        project_kernel,
        out_shape=jax.ShapeDtypeStruct((rows, columns), F32),
        in_specs=[SMEM] + [VMEM] * 5,
        out_specs=VMEM,
        compiler_params=PARAMS,
        cost_estimate=pl.CostEstimate(
            flops=2 * rows * 4096 * columns, bytes_accessed=4096 * 2 * (rows + columns), transcendentals=0
        ),
        name="project",
    )(order, tokens, *weights)


def short(proj, taps):
    n = proj.shape[0] - HALO
    return (
        taps[0:1] * proj[HALO : HALO + n]
        + taps[1:2] * proj[HALO - 1 : HALO - 1 + n]
        + taps[2:3] * proj[HALO - 2 : HALO - 2 + n]
    )


def drive_kernel(place, mine, theirs, key_taps, value_taps, weigh, step, driven, before, state):
    proj = (mine[...] + theirs[...]).astype(BF16).astype(F32)
    key = short(proj[:, :BLOCK], key_taps[...])
    value = short(proj[:, BLOCK:], value_taps[...])
    signal = key * value
    first, second = signal[:BLOCK], signal[BLOCK:]
    upper = place[0] == 1
    driven[...] = jnp.where(upper, second, first)
    for r in range(MODES):
        w = weigh[r]
        one = jnp.sum(w * first, axis=0, keepdims=True)
        two = jnp.sum(w * second, axis=0, keepdims=True)
        before[r : r + 1] = jnp.where(upper, one, 0.0)
        state[r : r + 1] = two + step[r : r + 1] * one


def drive(place, mine, theirs, key_taps, value_taps, weigh, step):
    return pl.pallas_call(
        drive_kernel,
        out_shape=(
            jax.ShapeDtypeStruct((BLOCK, BLOCK), F32),
            jax.ShapeDtypeStruct((MODES, BLOCK), F32),
            jax.ShapeDtypeStruct((MODES, BLOCK), F32),
        ),
        in_specs=[SMEM] + [VMEM] * 6,
        out_specs=(VMEM, VMEM, VMEM),
        compiler_params=PARAMS,
        name="drive",
    )(place, mine, theirs, key_taps, value_taps, weigh, step)


def near_kernel(driven, taps, gain, out, padded):
    signal = driven[...]
    padded[:BLOCK] = jnp.zeros((BLOCK, BLOCK), F32)
    padded[BLOCK:] = signal
    total = gain[...] * signal
    for s in range(BLOCK):
        low = s // 8 * 8
        part = taps[s : s + 1] * padded[BLOCK + low - s : 2 * BLOCK - s]
        if low:
            part = jnp.concatenate([jnp.zeros((low, BLOCK), F32), part], axis=0)
        total = total + part
    out[...] = total


def near(driven, taps, gain):
    return pl.pallas_call(
        near_kernel,
        out_shape=jax.ShapeDtypeStruct((BLOCK, BLOCK), F32),
        in_specs=[VMEM] * 3,
        out_specs=VMEM,
        scratch_shapes=[pltpu.VMEM((2 * BLOCK, BLOCK), F32)],
        compiler_params=PARAMS,
        cost_estimate=pl.CostEstimate(flops=2 * BLOCK**3, bytes_accessed=3 * BLOCK * BLOCK * 4, transcendentals=0),
        name="near",
    )(driven, taps, gain)


def finish_kernel(mine, theirs, query_taps, inner, reach, carry, out):
    proj = (mine[...] + theirs[...]).astype(BF16).astype(F32)
    query = short(proj, query_taps[...])
    conv = inner[...]
    for r in range(MODES):
        conv = conv + reach[r] * carry[r : r + 1]
    out[...] = (query * conv).T


def finish(mine, theirs, query_taps, inner, reach, carry):
    return pl.pallas_call(
        finish_kernel,
        out_shape=jax.ShapeDtypeStruct((BLOCK, BLOCK), F32),
        in_specs=[VMEM] * 6,
        out_specs=VMEM,
        compiler_params=PARAMS,
        name="finish",
    )(mine, theirs, query_taps, inner, reach, carry)


def body(tokens, in_weight, short_taps, residues, rates, skip_gain):
    place = lax.axis_index("ctx")
    tp = lax.axis_index("tp")
    core = place & 1
    chip_z, chip_x = (place >> 1) & 7, place >> 4
    tp_y, tp_h = tp & 3, tp >> 2

    rate = rates.T
    amount = residues.T * jnp.sqrt(2.0 * rate)
    index = jnp.arange(BLOCK, dtype=F32)[None, :, None]
    weigh = jnp.exp(-rate[:, None, :] * (BLOCK - 1.0 - index))
    reach = amount[:, None, :] * jnp.exp(-rate[:, None, :] * (index + 1.0))
    taps = jnp.sum(amount[:, None, :] * jnp.exp(-rate[:, None, :] * index), axis=0)
    step = jnp.exp(-rate * float(BLOCK))

    features = gather_tokens(tokens, core).reshape(16, HALO + 2 * BLOCK, 256)
    pair = gather_weights(jnp.concatenate([in_weight[1], in_weight[2]], axis=1), place)
    single = gather_weights(in_weight[0], place)

    turn = jnp.arange(16, dtype=jnp.int32)
    src_x = chip_x ^ (turn >> 2)
    src_z = (chip_z >> 1) ^ (((turn & 1) << 1) | ((turn >> 1) & 1))
    need_h = (src_x >> 1) ^ tp_h
    need_y = (((src_x & 1) << 1) | (src_z >> 1)) ^ tp_y
    order = (need_y << 2) | (need_h << 1) | (src_z & 1)

    mine = project(order, features, pair)
    theirs = flip(mine, "ctx", 1)
    driven, before, state = drive(
        core[None], mine, theirs, short_taps[1].T, short_taps[2].T, weigh, step
    )

    far = project(order, features, single)
    length = HALO + BLOCK
    own = lax.dynamic_slice_in_dim(far, core * BLOCK, length, 0)
    gift = lax.dynamic_slice_in_dim(far, (1 - core) * BLOCK, length, 0)
    other = flip(gift, "ctx", 1)

    inner = near(driven, taps, skip_gain[None])

    for bit in range(1, 6):
        group = 1 << bit
        upper = (place & group) == group
        past = flip(state, "ctx", group)
        whole = jnp.exp(-rate * float(BLOCK * group))
        since = jnp.exp(-rate * (BLOCK * (place & (group - 1))).astype(F32))
        before = before + jnp.where(upper, since * past, 0.0)
        if bit < 5:
            state = jnp.where(upper, state + whole * past, whole * state + past)

    return finish(own, other, short_taps[0].T, inner, reach, before)


def solution(mesh):
    in_specs = (
        P("ctx", "tp"),
        P(None, "ctx", "tp"),
        P(None, "tp", None),
        P("tp", None),
        P("tp", None),
        P("tp"),
    )
    return jax.shard_map(
        body, mesh=mesh, in_specs=in_specs, out_specs=P("tp", "ctx"), check_vma=False
    )
```

```python
import jax
import jax.numpy as jnp
from jax import lax
from jax.experimental import pallas as pl
from jax.experimental.pallas import tpu as pltpu
from jax.sharding import PartitionSpec as P

F32 = jnp.float32
BF16 = jnp.bfloat16
HALO = 16
BLOCK = 128
GROUP = 4 * BLOCK
ROWS = HALO + GROUP
PIECE = HALO + BLOCK
HALF = 80
MODES = 16
VMEM = pl.BlockSpec(memory_space=pltpu.VMEM)
SMEM = pl.BlockSpec(memory_space=pltpu.SMEM)
PARAMS = pltpu.CompilerParams(vmem_limit_bytes=48 * 1024 * 1024)


def flip(x, axis, mask):
    length = lax.axis_size(axis)
    return lax.ppermute(x, axis, [(i, i ^ mask) for i in range(length)])


def ahead(x, axis, by):
    length = lax.axis_size(axis)
    return lax.ppermute(x, axis, [(i, i + by) for i in range(length - by)])


def ordered(upper, own, other, axis):
    first = jnp.where(upper, other, own)
    second = jnp.where(upper, own, other)
    return jnp.concatenate([first, second], axis=axis)


def split_kernel(place, tokens, halo, kept, given):
    core = place[0] & 1
    for out, side in ((kept, core), (given, 1 - core)):
        for bit8 in range(2):
            for bit9 in range(2):
                start = pl.multiple_of(512 * bit9 + 256 * bit8 + side * 128, 128)
                there = slice(128 * bit9, 128 * bit9 + 128)
                out[bit8, :HALO, there] = halo[:, pl.ds(start, 128)]
                out[bit8, HALO:, there] = tokens[:, pl.ds(start, 128)]


def split(place, tokens, halo):
    shape = jax.ShapeDtypeStruct((2, PIECE, 256), BF16)
    return pl.pallas_call(
        split_kernel,
        out_shape=(shape, shape),
        in_specs=[SMEM, VMEM, VMEM],
        out_specs=(VMEM, VMEM),
        compiler_params=PARAMS,
        name="split",
    )(place, tokens, halo)


def joined(upper, own, other, axis):
    first = jnp.where(upper, other, own)
    second = jnp.where(upper, own, other)
    rest = lax.slice_in_dim(second, HALO, second.shape[axis], axis=axis)
    return jnp.concatenate([first, rest], axis=axis)


def gather_tokens(tokens, place):
    halo = ahead(tokens[BLOCK - HALO :], "ctx", 1)
    kept, given = split(place[None], tokens, halo)
    both = joined((place & 1) == 1, kept, flip(given, "ctx", 1), 1)
    upper = (place & 2) == 2
    keep = jnp.where(upper, both[1], both[0])
    give = jnp.where(upper, both[0], both[1])
    near_h = joined(upper, keep, flip(give, "ctx", 2), 0)
    far_h = flip(near_h, "tp", 4)
    found = []
    for part in (near_h, far_h):
        found += [part] + [flip(part, "tp", m) for m in (1, 2, 3)]
    return found


def gather_weights(piece, place):
    held = piece[None]
    held = jnp.concatenate([held, flip(held, "ctx", 8)], axis=0)
    held = ordered((place & 4) == 4, held, flip(held, "ctx", 4), 1)
    return [held] + [flip(held, "ctx", m << 4) for m in (1, 2, 3)]


def project_kernel(match, t0, t1, t2, t3, t4, t5, t6, t7, w0, w1, w2, w3, out):
    tokens, weights = (t0, t1, t2, t3, t4, t5, t6, t7), (w0, w1, w2, w3)
    for case in range(4):

        @pl.when(match[0] == case)
        def _():
            total = jnp.zeros(out.shape, F32)
            for turn in range(8):
                turn_h, turn_y = turn >> 2, turn & 3
                turn_x = case ^ (turn_h << 1 | turn_y >> 1)
                weight = weights[turn_x][match[1] ^ (turn_y & 1)]
                total += jnp.dot(tokens[turn][...], weight, preferred_element_type=F32)
            out[...] = total


def project(match, tokens, weights):
    columns = weights[0].shape[2]
    return pl.pallas_call(
        project_kernel,
        out_shape=jax.ShapeDtypeStruct((ROWS, columns), F32),
        in_specs=[SMEM] + [VMEM] * 12,
        out_specs=VMEM,
        compiler_params=PARAMS,
        cost_estimate=pl.CostEstimate(
            flops=2 * ROWS * 2048 * columns, bytes_accessed=2048 * 2 * (ROWS + columns), transcendentals=0
        ),
        name="project",
    )(match, *tokens, *weights)


def merge_kernel(place, mine, theirs, total, gift):
    total[...] = mine[...] + theirs[...]
    gift[:ROWS] = total[:, : 2 * BLOCK].astype(BF16)
    start = pl.multiple_of(((place[0] & 3) ^ 2) * BLOCK, BLOCK)
    gift[ROWS:, :BLOCK] = total[pl.ds(start, HALF), 2 * BLOCK :].astype(BF16)
    start = pl.multiple_of(start + PIECE - HALF, 16)
    gift[ROWS:, BLOCK:] = total[pl.ds(start, HALF), 2 * BLOCK :].astype(BF16)


def merge(place, mine, theirs):
    return pl.pallas_call(
        merge_kernel,
        out_shape=(
            jax.ShapeDtypeStruct(mine.shape, F32),
            jax.ShapeDtypeStruct((ROWS + HALF, 2 * BLOCK), BF16),
        ),
        in_specs=[SMEM, VMEM, VMEM],
        out_specs=(VMEM, VMEM),
        compiler_params=PARAMS,
        name="merge",
    )(place, mine, theirs)


def short(proj, taps):
    n = proj.shape[0] - HALO
    return (
        taps[0:1] * proj[HALO : HALO + n]
        + taps[1:2] * proj[HALO - 1 : HALO - 1 + n]
        + taps[2:3] * proj[HALO - 2 : HALO - 2 + n]
    )


def rounded(x):
    return x.astype(BF16).astype(F32)


def drive_kernel(place, mine, theirs, taps, weigh, step, query, driven, before, state, signal):
    spot = place[0] & 3
    pair = rounded(mine[:, : 2 * BLOCK] + theirs[:ROWS].astype(F32))
    key = short(pair[:, :BLOCK], taps[1])
    value = short(pair[:, BLOCK:], taps[2])
    signal[...] = key * value
    start = pl.multiple_of(spot * BLOCK, BLOCK)
    driven[...] = signal[pl.ds(start, BLOCK)]
    own = mine[pl.ds(start, PIECE), 2 * BLOCK :]
    other = theirs[ROWS:].astype(F32)
    other = jnp.concatenate([other[:, :BLOCK], other[2 * HALF - PIECE :, BLOCK:]], axis=0)
    query[...] = short(rounded(own + other), taps[0])
    for r in range(MODES):
        w, decay = weigh[r], step[r : r + 1]
        past = jnp.zeros((1, BLOCK), F32)
        held = past
        for b in range(4):
            held = jnp.where(spot == b, past, held)
            past = decay * past + jnp.sum(w * signal[BLOCK * b : BLOCK * b + BLOCK], axis=0, keepdims=True)
        before[r : r + 1] = held
        state[r : r + 1] = past


def drive(place, mine, theirs, taps, weigh, step):
    square = jax.ShapeDtypeStruct((BLOCK, BLOCK), F32)
    modes = jax.ShapeDtypeStruct((MODES, BLOCK), F32)
    return pl.pallas_call(
        drive_kernel,
        out_shape=(square, square, modes, modes),
        in_specs=[SMEM] + [VMEM] * 5,
        out_specs=(VMEM,) * 4,
        scratch_shapes=[pltpu.VMEM((GROUP, BLOCK), F32)],
        compiler_params=PARAMS,
        name="drive",
    )(place, mine, theirs, taps, weigh, step)


def near_kernel(driven, taps, gain, out, padded):
    signal = driven[...]
    padded[:BLOCK] = jnp.zeros((BLOCK, BLOCK), F32)
    padded[BLOCK:] = signal
    total = gain[...] * signal
    for s in range(BLOCK):
        low = s // 8 * 8
        part = taps[s : s + 1] * padded[BLOCK + low - s : 2 * BLOCK - s]
        if low:
            part = jnp.concatenate([jnp.zeros((low, BLOCK), F32), part], axis=0)
        total = total + part
    out[...] = total


def near(driven, taps, gain):
    return pl.pallas_call(
        near_kernel,
        out_shape=jax.ShapeDtypeStruct((BLOCK, BLOCK), F32),
        in_specs=[VMEM] * 3,
        out_specs=VMEM,
        scratch_shapes=[pltpu.VMEM((2 * BLOCK, BLOCK), F32)],
        compiler_params=PARAMS,
        cost_estimate=pl.CostEstimate(flops=2 * BLOCK**3, bytes_accessed=3 * BLOCK * BLOCK * 4, transcendentals=0),
        name="near",
    )(driven, taps, gain)


def finish_kernel(query, inner, reach, carry, out):
    conv = inner[...]
    for r in range(MODES):
        conv = conv + reach[r] * carry[r : r + 1]
    out[...] = (query[...] * conv).T


def finish(query, inner, reach, carry):
    return pl.pallas_call(
        finish_kernel,
        out_shape=jax.ShapeDtypeStruct((BLOCK, BLOCK), F32),
        in_specs=[VMEM] * 4,
        out_specs=VMEM,
        compiler_params=PARAMS,
        name="finish",
    )(query, inner, reach, carry)


def body(tokens, in_weight, short_taps, residues, rates, skip_gain):
    place = lax.axis_index("ctx")
    tp = lax.axis_index("tp")

    rate = rates.T
    amount = residues.T * jnp.sqrt(2.0 * rate)
    index = jnp.arange(BLOCK, dtype=F32)[None, :, None]
    weigh = jnp.exp(-rate[:, None, :] * (BLOCK - 1.0 - index))
    reach = amount[:, None, :] * jnp.exp(-rate[:, None, :] * (index + 1.0))
    taps = jnp.sum(amount[:, None, :] * jnp.exp(-rate[:, None, :] * index), axis=0)
    step = jnp.exp(-rate * float(BLOCK))

    weights = gather_weights(jnp.concatenate([in_weight[1], in_weight[2], in_weight[0]], axis=1), place)
    features = gather_tokens(tokens, place)
    apart = tp ^ (place >> 3)
    match = jnp.stack([apart >> 1, apart & 1])

    spot = place[None]
    mine = project(match, features, weights)
    total, gift = merge(spot, mine, flip(mine, "ctx", 1))
    theirs = flip(gift, "ctx", 2)
    short_rows = short_taps.transpose(0, 2, 1)
    query, driven, before, state = drive(spot, total, theirs, short_rows, weigh, step)
    inner = near(driven, taps, skip_gain[None])

    for bit in range(2, 6):
        size = 1 << bit
        upper = (place & size) == size
        past = flip(state, "ctx", size)
        whole = jnp.exp(-rate * float(BLOCK * size))
        since = jnp.exp(-rate * (BLOCK * (place & (size - 1))).astype(F32))
        before = before + jnp.where(upper, since * past, 0.0)
        if bit < 5:
            state = jnp.where(upper, state + whole * past, whole * state + past)

    return finish(query, inner, reach, before)


def solution(mesh):
    in_specs = (
        P("ctx", "tp"),
        P(None, "ctx", "tp"),
        P(None, "tp", None),
        P("tp", None),
        P("tp", None),
        P("tp"),
    )
    return jax.shard_map(
        body, mesh=mesh, in_specs=in_specs, out_specs=P("tp", "ctx"), check_vma=False
    )
```

```python
import jax
import jax.numpy as jnp
from jax import lax
from jax.experimental import pallas as pl
from jax.experimental.pallas import tpu as pltpu
from jax.sharding import PartitionSpec as P

F32 = jnp.float32
BF16 = jnp.bfloat16
HALO = 16
BLOCK = 128
GROUP = 4 * BLOCK
ROWS = HALO + GROUP
PIECE = HALO + BLOCK
OWN = 2 * PIECE
MODES = 16
VMEM = pl.BlockSpec(memory_space=pltpu.VMEM)
SMEM = pl.BlockSpec(memory_space=pltpu.SMEM)
PARAMS = pltpu.CompilerParams(vmem_limit_bytes=48 * 1024 * 1024)


def flip(x, axis, mask):
    length = lax.axis_size(axis)
    return lax.ppermute(x, axis, [(i, i ^ mask) for i in range(length)])


def ahead(x, axis, by):
    length = lax.axis_size(axis)
    return lax.ppermute(x, axis, [(i, i + by) for i in range(length - by)])


def ordered(upper, own, other, axis):
    first = jnp.where(upper, other, own)
    second = jnp.where(upper, own, other)
    return jnp.concatenate([first, second], axis=axis)


def flip_many(x, axis, masks):
    return [flip(x, axis, m) for m in masks]


def split_kernel(place, tokens, kept, given):
    core = place[0] & 1
    for out, side in ((kept, core), (given, 1 - core)):
        for bit8 in range(2):
            for bit9 in range(2):
                start = pl.multiple_of(512 * bit9 + 256 * bit8 + side * 128, 128)
                out[bit8, :, 128 * bit9 : 128 * bit9 + 128] = tokens[:, pl.ds(start, 128)]


def split(place, tokens):
    shape = jax.ShapeDtypeStruct((2, BLOCK, 256), BF16)
    return pl.pallas_call(
        split_kernel,
        out_shape=(shape, shape),
        in_specs=[SMEM, VMEM],
        out_specs=(VMEM, VMEM),
        compiler_params=PARAMS,
        name="split",
    )(place, tokens)


def gather(tokens, in_weight, place):
    kept, given = split(place[None], tokens)
    both = ordered((place & 1) == 1, kept, flip(given, "ctx", 1), 1)
    upper = (place & 2) == 2
    keep = jnp.where(upper, both[1], both[0])
    give = jnp.where(upper, both[0], both[1])
    keep, give, in_weight = lax.optimization_barrier((keep, give, in_weight))
    held = jnp.concatenate([in_weight[1], in_weight[2], in_weight[0]], axis=1)[None]
    near_h = ordered(upper, keep, flip(give, "ctx", 2), 0)
    past = flip(held, "ctx", 8)
    far_h = flip(near_h, "tp", 4)
    near_h, past = lax.optimization_barrier((near_h, past))
    halo = ahead(near_h[GROUP - HALO :], "ctx", 4)
    held = jnp.concatenate([held, past], axis=0)
    held = ordered((place & 4) == 4, held, flip(held, "ctx", 4), 1)
    far_halo = flip(halo, "tp", 4)
    found = []
    for part in (jnp.concatenate([halo, near_h]), jnp.concatenate([far_halo, far_h])):
        found += [part] + flip_many(part, "tp", (1, 2, 3))
    return found, [held] + flip_many(held, "ctx", (16, 32, 48))


def project_kernel(match, *refs):
    tokens, weights, kept, given, total = refs[:8], refs[8:12], refs[12], refs[13], refs[14]
    for case in range(4):

        @pl.when(match[0] == case)
        def _():
            added = jnp.zeros(total.shape, F32)
            for turn in range(8):
                turn_h, turn_y = turn >> 2, turn & 3
                turn_x = case ^ (turn_h << 1 | turn_y >> 1)
                weight = weights[turn_x][match[1] ^ (turn_y & 1)]
                added += jnp.dot(tokens[turn][...], weight, preferred_element_type=F32)
            total[...] = added

    for core in range(2):

        @pl.when(match[2] == core)
        def _():
            for out, side in ((kept, core), (given, 1 - core)):
                out[:ROWS] = total[:, BLOCK * side : BLOCK * side + BLOCK]
                for chip in range(2):
                    start = BLOCK * (2 * chip + side)
                    out[ROWS + PIECE * chip : ROWS + PIECE * chip + PIECE] = total[
                        start : start + PIECE, 2 * BLOCK :
                    ]


def project(match, tokens, weights):
    columns = weights[0].shape[2]
    shape = jax.ShapeDtypeStruct((ROWS + OWN, BLOCK), F32)
    return pl.pallas_call(
        project_kernel,
        out_shape=(shape, shape),
        in_specs=[SMEM] + [VMEM] * 12,
        out_specs=(VMEM, VMEM),
        scratch_shapes=[pltpu.VMEM((ROWS, columns), F32)],
        compiler_params=PARAMS,
        cost_estimate=pl.CostEstimate(
            flops=2 * ROWS * 2048 * columns, bytes_accessed=2048 * 2 * (ROWS + columns), transcendentals=0
        ),
        name="project",
    )(match, *tokens, *weights)


def merge_kernel(place, mine, theirs, pair, query, gift):
    pair[...] = mine[:ROWS] + theirs[:ROWS]
    gift[:ROWS] = pair[...]
    chip = (place[0] >> 1) & 1
    for out, first, side in ((query, 0, chip), (gift, ROWS, 1 - chip)):
        start = pl.multiple_of(ROWS + PIECE * side, 16)
        out[first : first + PIECE] = mine[pl.ds(start, PIECE)] + theirs[pl.ds(start, PIECE)]


def merge(place, mine, theirs):
    return pl.pallas_call(
        merge_kernel,
        out_shape=(
            jax.ShapeDtypeStruct((ROWS, BLOCK), F32),
            jax.ShapeDtypeStruct((PIECE, BLOCK), F32),
            jax.ShapeDtypeStruct((ROWS + PIECE, BLOCK), F32),
        ),
        in_specs=[SMEM, VMEM, VMEM],
        out_specs=(VMEM, VMEM, VMEM),
        compiler_params=PARAMS,
        name="merge",
    )(place, mine, theirs)


def short(proj, taps):
    n = proj.shape[0] - HALO
    return (
        taps[0:1] * proj[HALO : HALO + n]
        + taps[1:2] * proj[HALO - 1 : HALO - 1 + n]
        + taps[2:3] * proj[HALO - 2 : HALO - 2 + n]
    )


def drive_kernel(place, mine, theirs, own, other, taps, weigh, step, query, driven, before, state, signal):
    spot = place[0] & 3
    core = place[0] & 1
    first = jnp.where(core == 0, taps[1], taps[2])
    second = jnp.where(core == 0, taps[2], taps[1])
    signal[...] = short(mine[...].astype(F32), first) * short(theirs[...].astype(F32), second)
    start = pl.multiple_of(spot * BLOCK, BLOCK)
    driven[...] = signal[pl.ds(start, BLOCK)]
    query[...] = short((own[...] + other[...]).astype(BF16).astype(F32), taps[0])
    for r in range(MODES):
        w, decay = weigh[r], step[r : r + 1]
        past = jnp.zeros((1, BLOCK), F32)
        held = past
        for b in range(4):
            held = jnp.where(spot == b, past, held)
            past = decay * past + jnp.sum(w * signal[BLOCK * b : BLOCK * b + BLOCK], axis=0, keepdims=True)
        before[r : r + 1] = held
        state[r : r + 1] = past


def drive(place, mine, theirs, own, other, taps, weigh, step):
    square = jax.ShapeDtypeStruct((BLOCK, BLOCK), F32)
    modes = jax.ShapeDtypeStruct((MODES, BLOCK), F32)
    return pl.pallas_call(
        drive_kernel,
        out_shape=(square, square, modes, modes),
        in_specs=[SMEM] + [VMEM] * 7,
        out_specs=(VMEM,) * 4,
        scratch_shapes=[pltpu.VMEM((GROUP, BLOCK), F32)],
        compiler_params=PARAMS,
        name="drive",
    )(place, mine, theirs, own, other, taps, weigh, step)


def tables_kernel(place, residues, rates, weigh, reach, taps, step, toward, whole, last):
    at = place[0]
    index = lax.broadcasted_iota(jnp.int32, (BLOCK, BLOCK), 0).astype(F32)
    line = at & 15
    total = jnp.zeros((BLOCK, BLOCK), F32)
    for r in range(MODES):
        rate = rates[r : r + 1]
        amount = residues[r : r + 1] * jnp.sqrt(2.0 * rate)
        weigh[r] = jnp.exp(-rate * (BLOCK - 1.0 - index))
        reach[r] = amount * jnp.exp(-rate * (index + 1.0))
        total = total + amount * jnp.exp(-rate * index)
    taps[...] = total
    rate = rates[...]
    step[...] = jnp.exp(-rate * float(BLOCK))
    for turn in range(4):
        group = (line >> 2) ^ turn
        whole[turn] = jnp.exp(-rate * (GROUP * (3 - group)).astype(F32))
        if turn:
            for out, after in ((toward, line - 4 * (group + 1)), (last, at - 16 * (((at >> 4) ^ turn) + 1))):
                decay = jnp.exp(-rate * (BLOCK * jnp.maximum(after, 0)).astype(F32))
                out[turn - 1] = jnp.where(after >= 0, decay, 0.0)


def tables(place, residues, rates):
    def full(*shape):
        return jax.ShapeDtypeStruct(shape, F32)

    return pl.pallas_call(
        tables_kernel,
        out_shape=(
            full(MODES, BLOCK, BLOCK),
            full(MODES, BLOCK, BLOCK),
            full(BLOCK, BLOCK),
            full(MODES, BLOCK),
            full(3, MODES, BLOCK),
            full(4, MODES, BLOCK),
            full(3, MODES, BLOCK),
        ),
        in_specs=[SMEM, VMEM, VMEM],
        out_specs=(VMEM,) * 7,
        compiler_params=PARAMS,
        name="tables",
    )(place, residues, rates)


def advance_kernel(state, p1, p2, p3, before, toward, whole, out_before, out_state):
    out_before[...] = before[...] + toward[0] * p1[...] + toward[1] * p2[...] + toward[2] * p3[...]
    out_state[...] = whole[0] * state[...] + whole[1] * p1[...] + whole[2] * p2[...] + whole[3] * p3[...]


def advance(state, others, before, toward, whole):
    modes = jax.ShapeDtypeStruct((MODES, BLOCK), F32)
    return pl.pallas_call(
        advance_kernel,
        out_shape=(modes, modes),
        in_specs=[VMEM] * 7,
        out_specs=(VMEM, VMEM),
        compiler_params=PARAMS,
        name="advance",
    )(state, *others, before, toward, whole)


def near_kernel(driven, taps, gain, out, padded):
    signal = driven[...]
    padded[:BLOCK] = jnp.zeros((BLOCK, BLOCK), F32)
    padded[BLOCK:] = signal
    total = gain[...] * signal
    for s in range(BLOCK):
        low = s // 8 * 8
        part = taps[s : s + 1] * padded[BLOCK + low - s : 2 * BLOCK - s]
        if low:
            part = jnp.concatenate([jnp.zeros((low, BLOCK), F32), part], axis=0)
        total = total + part
    out[...] = total


def near(driven, taps, gain):
    return pl.pallas_call(
        near_kernel,
        out_shape=jax.ShapeDtypeStruct((BLOCK, BLOCK), F32),
        in_specs=[VMEM] * 3,
        out_specs=VMEM,
        scratch_shapes=[pltpu.VMEM((2 * BLOCK, BLOCK), F32)],
        compiler_params=PARAMS,
        cost_estimate=pl.CostEstimate(flops=2 * BLOCK**3, bytes_accessed=3 * BLOCK * BLOCK * 4, transcendentals=0),
        name="near",
    )(driven, taps, gain)


def finish_kernel(query, inner, reach, before, p1, p2, p3, last, out):
    carry = before[...] + last[0] * p1[...] + last[1] * p2[...] + last[2] * p3[...]
    conv = inner[...]
    for r in range(MODES):
        conv = conv + reach[r] * carry[r : r + 1]
    out[...] = (query[...] * conv).T


def finish(query, inner, reach, before, others, last):
    return pl.pallas_call(
        finish_kernel,
        out_shape=jax.ShapeDtypeStruct((BLOCK, BLOCK), F32),
        in_specs=[VMEM] * 8,
        out_specs=VMEM,
        compiler_params=PARAMS,
        name="finish",
    )(query, inner, reach, before, *others, last)


def body(tokens, in_weight, short_taps, residues, rates, skip_gain):
    place = lax.axis_index("ctx")
    tp = lax.axis_index("tp")
    spot = place[None]
    apart = tp ^ (place >> 3)
    match = jnp.stack([apart >> 1, apart & 1, place & 1])

    features, weights = gather(tokens, in_weight, place)
    weigh, reach, taps, step, toward, whole, last = tables(spot, residues.T, rates.T)

    mine, gift = project(match, features, weights)
    pair, own, gift = merge(spot, mine, flip(gift, "ctx", 1))
    theirs = flip(gift, "ctx", 2)
    mine = (pair + theirs[:ROWS]).astype(BF16)
    query, driven, before, state = drive(
        spot, mine, flip(mine, "ctx", 1), own, theirs[ROWS:], short_taps.transpose(0, 2, 1), weigh, step
    )
    others = flip_many(state, "ctx", (4, 8, 12))
    inner = near(driven, taps, skip_gain[None])
    before, state = advance(state, others, before, toward, whole)
    others = flip_many(state, "ctx", (16, 32, 48))
    return finish(query, inner, reach, before, others, last)


def solution(mesh):
    in_specs = (
        P("ctx", "tp"),
        P(None, "ctx", "tp"),
        P(None, "tp", None),
        P("tp", None),
        P("tp", None),
        P("tp"),
    )
    return jax.shard_map(
        body, mesh=mesh, in_specs=in_specs, out_specs=P("tp", "ctx"), check_vma=False
    )
```

```python
import jax
import jax.numpy as jnp
from jax import lax
from jax.experimental import pallas as pl
from jax.experimental.pallas import tpu as pltpu
from jax.sharding import PartitionSpec as P

F32 = jnp.float32
BF16 = jnp.bfloat16
HALO = 16
BLOCK = 128
GROUP = 4 * BLOCK
ROWS = HALO + GROUP
PIECE = HALO + BLOCK
OWN = 2 * PIECE
MODES = 16
VMEM = pl.BlockSpec(memory_space=pltpu.VMEM)
SMEM = pl.BlockSpec(memory_space=pltpu.SMEM)
PARAMS = pltpu.CompilerParams(vmem_limit_bytes=48 * 1024 * 1024)


def flip(x, axis, mask):
    length = lax.axis_size(axis)
    return lax.ppermute(x, axis, [(i, i ^ mask) for i in range(length)])


def ahead(x, axis, by):
    length = lax.axis_size(axis)
    return lax.ppermute(x, axis, [(i, i + by) for i in range(length - by)])


def ordered(upper, own, other, axis):
    first = jnp.where(upper, other, own)
    second = jnp.where(upper, own, other)
    return jnp.concatenate([first, second], axis=axis)


def share(x, axis, groups):
    size = len(groups[0])
    return swap(jnp.broadcast_to(x[None], (size,) + x.shape), axis, groups)


def swap(x, axis, groups):
    return lax.all_to_all(x, axis, 0, 0, axis_index_groups=groups)


NEIGHBOURS = [[4 * i + j for j in range(4)] for i in range(16)]
LINE = [[16 * x + 4 * i + low for i in range(4)] for x in range(4) for low in range(4)]
ACROSS = [[p + 16 * i for i in range(4)] for p in range(16)]
ROUND = [[0, 1, 2, 3], [4, 5, 6, 7]]


def flip_many(x, axis, masks):
    return [flip(x, axis, m) for m in masks]


def split_kernel(place, tokens, halo, kept, given):
    core = place[0] & 1
    for out, side in ((kept, core), (given, 1 - core)):
        for bit8 in range(2):
            for bit9 in range(2):
                start = pl.multiple_of(512 * bit9 + 256 * bit8 + side * 128, 128)
                there = slice(128 * bit9, 128 * bit9 + 128)
                out[bit8, :HALO, there] = halo[:, pl.ds(start, 128)]
                out[bit8, HALO:, there] = tokens[:, pl.ds(start, 128)]


def split(place, tokens, halo):
    shape = jax.ShapeDtypeStruct((2, PIECE, 256), BF16)
    return pl.pallas_call(
        split_kernel,
        out_shape=(shape, shape),
        in_specs=[SMEM, VMEM, VMEM],
        out_specs=(VMEM, VMEM),
        compiler_params=PARAMS,
        name="split",
    )(place, tokens, halo)


def joined(upper, own, other, axis):
    first = jnp.where(upper, other, own)
    second = jnp.where(upper, own, other)
    rest = lax.slice_in_dim(second, HALO, second.shape[axis], axis=axis)
    return jnp.concatenate([first, rest], axis=axis)


def gather(tokens, in_weight, place):
    held = jnp.concatenate([in_weight[1], in_weight[2], in_weight[0]], axis=1)[None]
    held = jnp.concatenate([held, flip(held, "ctx", 8)], axis=0)
    held = ordered((place & 4) == 4, held, flip(held, "ctx", 4), 1)
    weights = [held] + flip_many(held, "ctx", (16, 32, 48))
    halo = ahead(tokens[BLOCK - HALO :], "ctx", 1)
    kept, given = split(place[None], tokens, halo)
    both = joined((place & 1) == 1, kept, flip(given, "ctx", 1), 1)
    upper = (place & 2) == 2
    keep = jnp.where(upper, both[1], both[0])
    give = jnp.where(upper, both[0], both[1])
    near_h = joined(upper, keep, flip(give, "ctx", 2), 0)
    turns = [near_h] + flip_many(near_h, "tp", (1, 2, 3))
    far_h, turns, weights[2] = lax.optimization_barrier((flip(near_h, "tp", 4), turns, weights[2]))
    return turns, share(far_h, "tp", ROUND), weights


def project_kernel(match, t0, t1, t2, t3, far_h, w0, w1, w2, w3, kept, given, total):
    near_h, weights = (t0, t1, t2, t3), (w0, w1, w2, w3)
    for case in range(4):

        @pl.when(match[0] == case)
        def _():
            added = jnp.zeros(total.shape, F32)
            for turn in range(8):
                turn_h, turn_y = turn >> 2, turn & 3
                part = far_h[match[3] ^ turn_y] if turn_h else near_h[turn_y][...]
                turn_x = case ^ (turn_h << 1 | turn_y >> 1)
                weight = weights[turn_x][match[1] ^ (turn_y & 1)]
                added += jnp.dot(part, weight, preferred_element_type=F32)
            total[...] = added

    for core in range(2):

        @pl.when(match[2] == core)
        def _():
            for out, side in ((kept, core), (given, 1 - core)):
                out[:ROWS] = total[:, BLOCK * side : BLOCK * side + BLOCK]
                for chip in range(2):
                    start = BLOCK * (2 * chip + side)
                    out[ROWS + PIECE * chip : ROWS + PIECE * chip + PIECE] = total[
                        start : start + PIECE, 2 * BLOCK :
                    ]


def project(match, near_h, far_h, weights):
    columns = weights[0].shape[2]
    shape = jax.ShapeDtypeStruct((ROWS + OWN, BLOCK), F32)
    return pl.pallas_call(
        project_kernel,
        out_shape=(shape, shape),
        in_specs=[SMEM] + [VMEM] * 9,
        out_specs=(VMEM, VMEM),
        scratch_shapes=[pltpu.VMEM((ROWS, columns), F32)],
        compiler_params=PARAMS,
        cost_estimate=pl.CostEstimate(
            flops=2 * ROWS * 2048 * columns, bytes_accessed=2048 * 2 * (ROWS + columns), transcendentals=0
        ),
        name="project",
    )(match, *near_h, far_h, *weights)


def merge_kernel(place, mine, theirs, pair, query, gift):
    pair[...] = mine[:ROWS] + theirs[:ROWS]
    gift[:ROWS] = pair[...]
    chip = (place[0] >> 1) & 1
    for out, first, side in ((query, 0, chip), (gift, ROWS, 1 - chip)):
        start = pl.multiple_of(ROWS + PIECE * side, 16)
        out[first : first + PIECE] = mine[pl.ds(start, PIECE)] + theirs[pl.ds(start, PIECE)]


def merge(place, mine, theirs):
    return pl.pallas_call(
        merge_kernel,
        out_shape=(
            jax.ShapeDtypeStruct((ROWS, BLOCK), F32),
            jax.ShapeDtypeStruct((PIECE, BLOCK), F32),
            jax.ShapeDtypeStruct((ROWS + PIECE, BLOCK), F32),
        ),
        in_specs=[SMEM, VMEM, VMEM],
        out_specs=(VMEM, VMEM, VMEM),
        compiler_params=PARAMS,
        name="merge",
    )(place, mine, theirs)


def short(proj, taps):
    n = proj.shape[0] - HALO
    return (
        taps[0:1] * proj[HALO : HALO + n]
        + taps[1:2] * proj[HALO - 1 : HALO - 1 + n]
        + taps[2:3] * proj[HALO - 2 : HALO - 2 + n]
    )


def drive_kernel(place, mine, theirs, own, other, taps, weigh, step, query, driven, before, state, signal):
    spot = place[0] & 3
    core = place[0] & 1
    first = jnp.where(core == 0, taps[1], taps[2])
    second = jnp.where(core == 0, taps[2], taps[1])
    signal[...] = short(mine[...].astype(F32), first) * short(theirs[...].astype(F32), second)
    start = pl.multiple_of(spot * BLOCK, BLOCK)
    driven[...] = signal[pl.ds(start, BLOCK)]
    query[...] = short((own[...] + other[...]).astype(BF16).astype(F32), taps[0])
    for r in range(MODES):
        w, decay = weigh[r], step[r : r + 1]
        past = jnp.zeros((1, BLOCK), F32)
        held = past
        for b in range(4):
            held = jnp.where(spot == b, past, held)
            past = decay * past + jnp.sum(w * signal[BLOCK * b : BLOCK * b + BLOCK], axis=0, keepdims=True)
        before[r : r + 1] = held
        for i in range(4):
            state[i, r : r + 1] = past


def drive(place, mine, theirs, own, other, taps, weigh, step):
    square = jax.ShapeDtypeStruct((BLOCK, BLOCK), F32)
    modes = jax.ShapeDtypeStruct((MODES, BLOCK), F32)
    copies = jax.ShapeDtypeStruct((4, MODES, BLOCK), F32)
    return pl.pallas_call(
        drive_kernel,
        out_shape=(square, square, modes, copies),
        in_specs=[SMEM] + [VMEM] * 7,
        out_specs=(VMEM,) * 4,
        scratch_shapes=[pltpu.VMEM((GROUP, BLOCK), F32)],
        compiler_params=PARAMS,
        name="drive",
    )(place, mine, theirs, own, other, taps, weigh, step)


def tables_kernel(place, residues, rates, weigh, reach, taps, step, toward, whole, last):
    at = place[0]
    index = lax.broadcasted_iota(jnp.int32, (BLOCK, BLOCK), 0).astype(F32)
    line = at & 15
    total = jnp.zeros((BLOCK, BLOCK), F32)
    for r in range(MODES):
        rate = rates[r : r + 1]
        amount = residues[r : r + 1] * jnp.sqrt(2.0 * rate)
        weigh[r] = jnp.exp(-rate * (BLOCK - 1.0 - index))
        reach[r] = amount * jnp.exp(-rate * (index + 1.0))
        total = total + amount * jnp.exp(-rate * index)
    taps[...] = total
    rate = rates[...]
    step[...] = jnp.exp(-rate * float(BLOCK))
    for i in range(4):
        whole[i] = jnp.exp(-rate * float(GROUP * (3 - i)))
        for out, after in ((toward, line - 4 * (i + 1)), (last, at - 16 * (i + 1))):
            decay = jnp.exp(-rate * (BLOCK * jnp.maximum(after, 0)).astype(F32))
            out[i] = jnp.where(after >= 0, decay, 0.0)


def tables(place, residues, rates):
    def full(*shape):
        return jax.ShapeDtypeStruct(shape, F32)

    return pl.pallas_call(
        tables_kernel,
        out_shape=(
            full(MODES, BLOCK, BLOCK),
            full(MODES, BLOCK, BLOCK),
            full(BLOCK, BLOCK),
            full(MODES, BLOCK),
            full(4, MODES, BLOCK),
            full(4, MODES, BLOCK),
            full(4, MODES, BLOCK),
        ),
        in_specs=[SMEM, VMEM, VMEM],
        out_specs=(VMEM,) * 7,
        compiler_params=PARAMS,
        name="tables",
    )(place, residues, rates)


def advance_kernel(states, before, toward, whole, out_before, out_state):
    held, total = before[...], jnp.zeros((MODES, BLOCK), F32)
    for i in range(4):
        held = held + toward[i] * states[i]
        total = total + whole[i] * states[i]
    out_before[...] = held
    for i in range(4):
        out_state[i] = total


def advance(states, before, toward, whole):
    modes = jax.ShapeDtypeStruct((MODES, BLOCK), F32)
    copies = jax.ShapeDtypeStruct((4, MODES, BLOCK), F32)
    return pl.pallas_call(
        advance_kernel,
        out_shape=(modes, copies),
        in_specs=[VMEM] * 4,
        out_specs=(VMEM, VMEM),
        compiler_params=PARAMS,
        name="advance",
    )(states, before, toward, whole)


def near_kernel(driven, taps, gain, out, padded):
    signal = driven[...]
    padded[:BLOCK] = jnp.zeros((BLOCK, BLOCK), F32)
    padded[BLOCK:] = signal
    total = gain[...] * signal
    for s in range(BLOCK):
        low = s // 8 * 8
        part = taps[s : s + 1] * padded[BLOCK + low - s : 2 * BLOCK - s]
        if low:
            part = jnp.concatenate([jnp.zeros((low, BLOCK), F32), part], axis=0)
        total = total + part
    out[...] = total


def near(driven, taps, gain):
    return pl.pallas_call(
        near_kernel,
        out_shape=jax.ShapeDtypeStruct((BLOCK, BLOCK), F32),
        in_specs=[VMEM] * 3,
        out_specs=VMEM,
        scratch_shapes=[pltpu.VMEM((2 * BLOCK, BLOCK), F32)],
        compiler_params=PARAMS,
        cost_estimate=pl.CostEstimate(flops=2 * BLOCK**3, bytes_accessed=3 * BLOCK * BLOCK * 4, transcendentals=0),
        name="near",
    )(driven, taps, gain)


def finish_kernel(query, inner, reach, before, states, last, out):
    carry = before[...]
    for i in range(4):
        carry = carry + last[i] * states[i]
    conv = inner[...]
    for r in range(MODES):
        conv = conv + reach[r] * carry[r : r + 1]
    out[...] = (query[...] * conv).T


def finish(query, inner, reach, before, states, last):
    return pl.pallas_call(
        finish_kernel,
        out_shape=jax.ShapeDtypeStruct((BLOCK, BLOCK), F32),
        in_specs=[VMEM] * 6,
        out_specs=VMEM,
        compiler_params=PARAMS,
        name="finish",
    )(query, inner, reach, before, states, last)


def body(tokens, in_weight, short_taps, residues, rates, skip_gain):
    place = lax.axis_index("ctx")
    tp = lax.axis_index("tp")
    spot = place[None]
    apart = tp ^ (place >> 3)
    match = jnp.stack([apart >> 1, apart & 1, place & 1, tp & 3])

    near_h, far_h, weights = gather(tokens, in_weight, place)
    weigh, reach, taps, step, toward, whole, last = tables(spot, residues.T, rates.T)

    mine, gift = project(match, near_h, far_h, weights)
    pair, own, gift = merge(spot, mine, flip(gift, "ctx", 1))
    theirs = flip(gift, "ctx", 2)
    mine = (pair + theirs[:ROWS]).astype(BF16)
    query, driven, before, state = drive(
        spot, mine, flip(mine, "ctx", 1), own, theirs[ROWS:], short_taps.transpose(0, 2, 1), weigh, step
    )
    inner = near(driven, taps, skip_gain[None])
    before, state = advance(swap(state, "ctx", LINE), before, toward, whole)
    return finish(query, inner, reach, before, swap(state, "ctx", ACROSS), last)


def solution(mesh):
    in_specs = (
        P("ctx", "tp"),
        P(None, "ctx", "tp"),
        P(None, "tp", None),
        P("tp", None),
        P("tp", None),
        P("tp"),
    )
    return jax.shard_map(
        body, mesh=mesh, in_specs=in_specs, out_specs=P("tp", "ctx"), check_vma=False
    )
```

```python
import jax
import jax.numpy as jnp
from jax import lax
from jax.experimental import pallas as pl
from jax.experimental.pallas import tpu as pltpu
from jax.sharding import PartitionSpec as P

F32 = jnp.float32
BF16 = jnp.bfloat16
HALO = 16
BLOCK = 128
GROUP = 4 * BLOCK
ROWS = HALO + GROUP
PIECE = HALO + BLOCK
OWN = 2 * PIECE
MODES = 16
VMEM = pl.BlockSpec(memory_space=pltpu.VMEM)
SMEM = pl.BlockSpec(memory_space=pltpu.SMEM)
PARAMS = pltpu.CompilerParams(vmem_limit_bytes=48 * 1024 * 1024)


def flip(x, axis, mask):
    length = lax.axis_size(axis)
    return lax.ppermute(x, axis, [(i, i ^ mask) for i in range(length)])


def ahead(x, axis, by):
    length = lax.axis_size(axis)
    return lax.ppermute(x, axis, [(i, i + by) for i in range(length - by)])


def ordered(upper, own, other, axis):
    first = jnp.where(upper, other, own)
    second = jnp.where(upper, own, other)
    return jnp.concatenate([first, second], axis=axis)


def share(x, axis, groups):
    size = len(groups[0])
    return swap(jnp.broadcast_to(x[None], (size,) + x.shape), axis, groups)


def swap(x, axis, groups):
    return lax.all_to_all(x, axis, 0, 0, axis_index_groups=groups)


NEIGHBOURS = [[4 * i + j for j in range(4)] for i in range(16)]
GROUPS = [[4 * i + low for i in range(16)] for low in range(4)]
ROUND = [[0, 1, 2, 3], [4, 5, 6, 7]]


def flip_many(x, axis, masks):
    return [flip(x, axis, m) for m in masks]


def split_kernel(place, tokens, halo, kept, given):
    core = place[0] & 1
    for out, side in ((kept, core), (given, 1 - core)):
        for bit8 in range(2):
            for bit9 in range(2):
                start = pl.multiple_of(512 * bit9 + 256 * bit8 + side * 128, 128)
                there = slice(128 * bit9, 128 * bit9 + 128)
                out[bit8, :HALO, there] = halo[:, pl.ds(start, 128)]
                out[bit8, HALO:, there] = tokens[:, pl.ds(start, 128)]


def split(place, tokens, halo):
    shape = jax.ShapeDtypeStruct((2, PIECE, 256), BF16)
    return pl.pallas_call(
        split_kernel,
        out_shape=(shape, shape),
        in_specs=[SMEM, VMEM, VMEM],
        out_specs=(VMEM, VMEM),
        compiler_params=PARAMS,
        name="split",
    )(place, tokens, halo)


def joined(upper, own, other, axis):
    first = jnp.where(upper, other, own)
    second = jnp.where(upper, own, other)
    rest = lax.slice_in_dim(second, HALO, second.shape[axis], axis=axis)
    return jnp.concatenate([first, rest], axis=axis)


def gather(tokens, in_weight, place):
    held = jnp.concatenate([in_weight[1], in_weight[2], in_weight[0]], axis=1)[None]
    held = jnp.concatenate([held, flip(held, "ctx", 8)], axis=0)
    held = ordered((place & 4) == 4, held, flip(held, "ctx", 4), 1)
    weights = [held] + flip_many(held, "ctx", (16, 32, 48))
    halo = ahead(tokens[BLOCK - HALO :], "ctx", 1)
    kept, given = split(place[None], tokens, halo)
    both = joined((place & 1) == 1, kept, flip(given, "ctx", 1), 1)
    upper = (place & 2) == 2
    keep = jnp.where(upper, both[1], both[0])
    give = jnp.where(upper, both[0], both[1])
    near_h = joined(upper, keep, flip(give, "ctx", 2), 0)
    turns = [near_h] + flip_many(near_h, "tp", (1, 2, 3))
    far_h, turns, weights[2] = lax.optimization_barrier((flip(near_h, "tp", 4), turns, weights[2]))
    return turns, share(far_h, "tp", ROUND), weights


def project_kernel(match, t0, t1, t2, t3, far_ref, w0, w1, w2, w3, kept, given, total, far_h, landed):
    bring = pltpu.make_async_copy(far_ref, far_h, landed)
    bring.start()
    near_h, weights = (t0, t1, t2, t3), (w0, w1, w2, w3)

    def half(case, turn_h):
        added = jnp.zeros(total.shape, F32)
        for turn_y in range(4):
            part = far_h[match[3] ^ turn_y] if turn_h else near_h[turn_y][...]
            turn_x = case ^ (turn_h << 1 | turn_y >> 1)
            weight = weights[turn_x][match[1] ^ (turn_y & 1)]
            added += jnp.dot(part, weight, preferred_element_type=F32)
        return added

    for case in range(4):

        @pl.when(match[0] == case)
        def _():
            total[...] = half(case, 0)

    bring.wait()
    for case in range(4):

        @pl.when(match[0] == case)
        def _():
            total[...] += half(case, 1)

    for core in range(2):

        @pl.when(match[2] == core)
        def _():
            for out, side in ((kept, core), (given, 1 - core)):
                out[:ROWS] = total[:, BLOCK * side : BLOCK * side + BLOCK]
                for chip in range(2):
                    start = BLOCK * (2 * chip + side)
                    out[ROWS + PIECE * chip : ROWS + PIECE * chip + PIECE] = total[
                        start : start + PIECE, 2 * BLOCK :
                    ]


def project(match, near_h, far_h, weights):
    columns = weights[0].shape[2]
    shape = jax.ShapeDtypeStruct((ROWS + OWN, BLOCK), F32)
    return pl.pallas_call(
        project_kernel,
        out_shape=(shape, shape),
        in_specs=[SMEM] + [VMEM] * 4 + [pl.BlockSpec(memory_space=pl.ANY)] + [VMEM] * 4,
        out_specs=(VMEM, VMEM),
        scratch_shapes=[
            pltpu.VMEM((ROWS, columns), F32),
            pltpu.VMEM(far_h.shape, BF16),
            pltpu.SemaphoreType.DMA(()),
        ],
        compiler_params=PARAMS,
        cost_estimate=pl.CostEstimate(
            flops=2 * ROWS * 2048 * columns, bytes_accessed=2048 * 2 * (ROWS + columns), transcendentals=0
        ),
        name="project",
    )(match, *near_h, far_h, *weights)


def merge_kernel(place, mine, theirs, pair, query, gift):
    pair[...] = mine[:ROWS] + theirs[:ROWS]
    chip = (place[0] >> 1) & 1
    for out, side in ((query, chip), (gift, 1 - chip)):
        start = pl.multiple_of(ROWS + PIECE * side, 16)
        out[...] = mine[pl.ds(start, PIECE)] + theirs[pl.ds(start, PIECE)]


def merge(place, mine, theirs):
    piece = jax.ShapeDtypeStruct((PIECE, BLOCK), F32)
    return pl.pallas_call(
        merge_kernel,
        out_shape=(jax.ShapeDtypeStruct((ROWS, BLOCK), F32), piece, piece),
        in_specs=[SMEM, VMEM, VMEM],
        out_specs=(VMEM, VMEM, VMEM),
        compiler_params=PARAMS,
        name="merge",
    )(place, mine, theirs)


def short(proj, taps):
    n = proj.shape[0] - HALO
    return (
        taps[0:1] * proj[HALO : HALO + n]
        + taps[1:2] * proj[HALO - 1 : HALO - 1 + n]
        + taps[2:3] * proj[HALO - 2 : HALO - 2 + n]
    )


def drive_kernel(place, mine, theirs, taps, weigh, step, driven, before, state, signal, total):
    spot = place[0] & 3
    core = place[0] & 1
    first = jnp.where(core == 0, taps[1], taps[2])
    second = jnp.where(core == 0, taps[2], taps[1])
    signal[...] = short(mine[...].astype(F32), first) * short(theirs[...].astype(F32), second)
    start = pl.multiple_of(spot * BLOCK, BLOCK)
    driven[...] = signal[pl.ds(start, BLOCK)]
    for r in range(MODES):
        w, decay = weigh[r], step[r : r + 1]
        past = jnp.zeros((1, BLOCK), F32)
        held = past
        for b in range(4):
            held = jnp.where(spot == b, past, held)
            past = decay * past + jnp.sum(w * signal[BLOCK * b : BLOCK * b + BLOCK], axis=0, keepdims=True)
        before[r : r + 1] = held
        total[r : r + 1] = past
    for i in range(16):
        state[i] = total[...]


def drive(place, mine, theirs, taps, weigh, step):
    square = jax.ShapeDtypeStruct((BLOCK, BLOCK), F32)
    modes = jax.ShapeDtypeStruct((MODES, BLOCK), F32)
    copies = jax.ShapeDtypeStruct((16, MODES, BLOCK), F32)
    return pl.pallas_call(
        drive_kernel,
        out_shape=(square, modes, copies),
        in_specs=[SMEM] + [VMEM] * 5,
        out_specs=(VMEM,) * 3,
        scratch_shapes=[pltpu.VMEM((GROUP, BLOCK), F32), pltpu.VMEM((MODES, BLOCK), F32)],
        compiler_params=PARAMS,
        name="drive",
    )(place, mine, theirs, taps, weigh, step)


def tables_kernel(place, residues, rates, weigh, reach, taps, step, last):
    at = place[0]
    index = lax.broadcasted_iota(jnp.int32, (BLOCK, BLOCK), 0).astype(F32)
    total = jnp.zeros((BLOCK, BLOCK), F32)
    for r in range(MODES):
        rate = rates[r : r + 1]
        amount = residues[r : r + 1] * jnp.sqrt(2.0 * rate)
        weigh[r] = jnp.exp(-rate * (BLOCK - 1.0 - index))
        reach[r] = amount * jnp.exp(-rate * (index + 1.0))
        total = total + amount * jnp.exp(-rate * index)
    taps[...] = total
    rate = rates[...]
    step[...] = jnp.exp(-rate * float(BLOCK))
    for i in range(16):
        after = at - 4 * (i + 1)
        decay = jnp.exp(-rate * (BLOCK * jnp.maximum(after, 0)).astype(F32))
        last[i] = jnp.where(after >= 0, decay, 0.0)


def tables(place, residues, rates):
    def full(*shape):
        return jax.ShapeDtypeStruct(shape, F32)

    return pl.pallas_call(
        tables_kernel,
        out_shape=(
            full(MODES, BLOCK, BLOCK),
            full(MODES, BLOCK, BLOCK),
            full(BLOCK, BLOCK),
            full(MODES, BLOCK),
            full(16, MODES, BLOCK),
        ),
        in_specs=[SMEM, VMEM, VMEM],
        out_specs=(VMEM,) * 5,
        compiler_params=PARAMS,
        name="tables",
    )(place, residues, rates)


def near_kernel(driven, taps, gain, out, padded):
    signal = driven[...]
    padded[:BLOCK] = jnp.zeros((BLOCK, BLOCK), F32)
    padded[BLOCK:] = signal
    total = gain[...] * signal
    for s in range(BLOCK):
        low = s // 8 * 8
        part = taps[s : s + 1] * padded[BLOCK + low - s : 2 * BLOCK - s]
        if low:
            part = jnp.concatenate([jnp.zeros((low, BLOCK), F32), part], axis=0)
        total = total + part
    out[...] = total


def near(driven, taps, gain):
    return pl.pallas_call(
        near_kernel,
        out_shape=jax.ShapeDtypeStruct((BLOCK, BLOCK), F32),
        in_specs=[VMEM] * 3,
        out_specs=VMEM,
        scratch_shapes=[pltpu.VMEM((2 * BLOCK, BLOCK), F32)],
        compiler_params=PARAMS,
        cost_estimate=pl.CostEstimate(flops=2 * BLOCK**3, bytes_accessed=3 * BLOCK * BLOCK * 4, transcendentals=0),
        name="near",
    )(driven, taps, gain)


def finish_kernel(own, other, taps, inner, reach, before, states, last, out):
    query = short((own[...] + other[...]).astype(BF16).astype(F32), taps[0])
    carry = before[...]
    for i in range(16):
        carry = carry + last[i] * states[i]
    conv = inner[...]
    for r in range(MODES):
        conv = conv + reach[r] * carry[r : r + 1]
    out[...] = (query * conv).T


def finish(own, other, taps, inner, reach, before, states, last):
    return pl.pallas_call(
        finish_kernel,
        out_shape=jax.ShapeDtypeStruct((BLOCK, BLOCK), F32),
        in_specs=[VMEM] * 8,
        out_specs=VMEM,
        compiler_params=PARAMS,
        name="finish",
    )(own, other, taps, inner, reach, before, states, last)


def body(tokens, in_weight, short_taps, residues, rates, skip_gain):
    place = lax.axis_index("ctx")
    tp = lax.axis_index("tp")
    spot = place[None]
    apart = tp ^ (place >> 3)
    match = jnp.stack([apart >> 1, apart & 1, place & 1, tp & 3])

    near_h, far_h, weights = gather(tokens, in_weight, place)
    weigh, reach, taps, step, last = tables(spot, residues.T, rates.T)

    mine, gift = project(match, near_h, far_h, weights)
    pair, own, gift = merge(spot, mine, flip(gift, "ctx", 1))
    mine = (pair + flip(pair, "ctx", 2)).astype(BF16)
    other = flip(gift, "ctx", 2)
    short_rows = short_taps.transpose(0, 2, 1)
    driven, before, state = drive(spot, mine, flip(mine, "ctx", 1), short_rows, weigh, step)
    inner = near(driven, taps, skip_gain[None])
    return finish(own, other, short_rows, inner, reach, before, swap(state, "ctx", GROUPS), last)


def solution(mesh):
    in_specs = (
        P("ctx", "tp"),
        P(None, "ctx", "tp"),
        P(None, "tp", None),
        P("tp", None),
        P("tp", None),
        P("tp"),
    )
    return jax.shard_map(
        body, mesh=mesh, in_specs=in_specs, out_specs=P("tp", "ctx"), check_vma=False
    )
```

```python
import jax
import jax.numpy as jnp
from jax import lax
from jax.experimental import pallas as pl
from jax.experimental.pallas import tpu as pltpu
from jax.sharding import PartitionSpec as P

F32 = jnp.float32
BF16 = jnp.bfloat16
HALO = 16
BLOCK = 128
GROUP = 4 * BLOCK
ROWS = HALO + GROUP
PIECE = HALO + BLOCK
OWN = 2 * PIECE
MODES = 16
VMEM = pl.BlockSpec(memory_space=pltpu.VMEM)
SMEM = pl.BlockSpec(memory_space=pltpu.SMEM)
PARAMS = pltpu.CompilerParams(vmem_limit_bytes=48 * 1024 * 1024)


def flip(x, axis, mask):
    length = lax.axis_size(axis)
    return lax.ppermute(x, axis, [(i, i ^ mask) for i in range(length)])


def ahead(x, axis, by):
    length = lax.axis_size(axis)
    return lax.ppermute(x, axis, [(i, i + by) for i in range(length - by)])


def ordered(upper, own, other, axis):
    first = jnp.where(upper, other, own)
    second = jnp.where(upper, own, other)
    return jnp.concatenate([first, second], axis=axis)


def share(x, axis, groups):
    size = len(groups[0])
    return swap(jnp.broadcast_to(x[None], (size,) + x.shape), axis, groups)


def swap(x, axis, groups):
    return lax.all_to_all(x, axis, 0, 0, axis_index_groups=groups)


NEIGHBOURS = [[4 * i + j for j in range(4)] for i in range(16)]
GROUPS = [[4 * i + low for i in range(16)] for low in range(4)]
ROUND = [[0, 1, 2, 3], [4, 5, 6, 7]]


def flip_many(x, axis, masks):
    return [flip(x, axis, m) for m in masks]


def split_kernel(place, tokens, halo, kept, given):
    core = place[0] & 1
    for out, side in ((kept, core), (given, 1 - core)):
        for bit8 in range(2):
            for bit9 in range(2):
                start = pl.multiple_of(512 * bit9 + 256 * bit8 + side * 128, 128)
                there = slice(128 * bit9, 128 * bit9 + 128)
                out[bit8, :HALO, there] = halo[:, pl.ds(start, 128)]
                out[bit8, HALO:, there] = tokens[:, pl.ds(start, 128)]


def split(place, tokens, halo):
    shape = jax.ShapeDtypeStruct((2, PIECE, 256), BF16)
    return pl.pallas_call(
        split_kernel,
        out_shape=(shape, shape),
        in_specs=[SMEM, VMEM, VMEM],
        out_specs=(VMEM, VMEM),
        compiler_params=PARAMS,
        name="split",
    )(place, tokens, halo)


def joined(upper, own, other, axis):
    first = jnp.where(upper, other, own)
    second = jnp.where(upper, own, other)
    rest = lax.slice_in_dim(second, HALO, second.shape[axis], axis=axis)
    return jnp.concatenate([first, rest], axis=axis)


def gather(tokens, in_weight, place):
    held = jnp.concatenate([in_weight[1], in_weight[2], in_weight[0]], axis=1)[None]
    held = jnp.concatenate([held, flip(held, "ctx", 8)], axis=0)
    held = ordered((place & 4) == 4, held, flip(held, "ctx", 4), 1)
    weights = [held] + flip_many(held, "ctx", (16, 32, 48))
    halo = ahead(tokens[BLOCK - HALO :], "ctx", 1)
    kept, given = split(place[None], tokens, halo)
    both = joined((place & 1) == 1, kept, flip(given, "ctx", 1), 1)
    upper = (place & 2) == 2
    keep = jnp.where(upper, both[1], both[0])
    give = jnp.where(upper, both[0], both[1])
    near_h = joined(upper, keep, flip(give, "ctx", 2), 0)
    turns = [near_h] + flip_many(near_h, "tp", (1, 2, 3))
    far_h, turns[:3] = lax.optimization_barrier((flip(near_h, "tp", 4), turns[:3]))
    return turns, share(far_h, "tp", ROUND), weights


def project_kernel(match, t0, t1, t2, t3, far_ref, w0, w1, w2, w3, kept, given, total, far_h, t3_here, landed):
    bring = pltpu.make_async_copy(far_ref, far_h, landed.at[0])
    bring.start()
    also = pltpu.make_async_copy(t3, t3_here, landed.at[1])
    also.start()
    near_h, weights = (t0, t1, t2, t3_here), (w0, w1, w2, w3)

    def some(case, turn_h, turns):
        added = jnp.zeros(total.shape, F32)
        for turn_y in turns:
            part = far_h[match[3] ^ turn_y] if turn_h else near_h[turn_y][...]
            turn_x = case ^ (turn_h << 1 | turn_y >> 1)
            weight = weights[turn_x][match[1] ^ (turn_y & 1)]
            added += jnp.dot(part, weight, preferred_element_type=F32)
        return added

    for case in range(4):

        @pl.when(match[0] == case)
        def _():
            total[...] = some(case, 0, (0, 1, 2))

    also.wait()
    bring.wait()
    for case in range(4):

        @pl.when(match[0] == case)
        def _():
            total[...] += some(case, 0, (3,)) + some(case, 1, (0, 1, 2, 3))

    for core in range(2):

        @pl.when(match[2] == core)
        def _():
            for out, side in ((kept, core), (given, 1 - core)):
                out[:ROWS] = total[:, BLOCK * side : BLOCK * side + BLOCK]
                for chip in range(2):
                    start = BLOCK * (2 * chip + side)
                    out[ROWS + PIECE * chip : ROWS + PIECE * chip + PIECE] = total[
                        start : start + PIECE, 2 * BLOCK :
                    ]


def project(match, near_h, far_h, weights):
    columns = weights[0].shape[2]
    shape = jax.ShapeDtypeStruct((ROWS + OWN, BLOCK), F32)
    return pl.pallas_call(
        project_kernel,
        out_shape=(shape, shape),
        in_specs=[SMEM] + [VMEM] * 3 + [pl.BlockSpec(memory_space=pl.ANY)] * 2 + [VMEM] * 4,
        out_specs=(VMEM, VMEM),
        scratch_shapes=[
            pltpu.VMEM((ROWS, columns), F32),
            pltpu.VMEM(far_h.shape, BF16),
            pltpu.VMEM(far_h.shape[1:], BF16),
            pltpu.SemaphoreType.DMA((2,)),
        ],
        compiler_params=PARAMS,
        cost_estimate=pl.CostEstimate(
            flops=2 * ROWS * 2048 * columns, bytes_accessed=2048 * 2 * (ROWS + columns), transcendentals=0
        ),
        name="project",
    )(match, *near_h, far_h, *weights)


def merge_kernel(place, mine, theirs, pair, query, gift):
    pair[...] = mine[:ROWS] + theirs[:ROWS]
    chip = (place[0] >> 1) & 1
    for out, side in ((query, chip), (gift, 1 - chip)):
        start = pl.multiple_of(ROWS + PIECE * side, 16)
        out[...] = mine[pl.ds(start, PIECE)] + theirs[pl.ds(start, PIECE)]


def merge(place, mine, theirs):
    piece = jax.ShapeDtypeStruct((PIECE, BLOCK), F32)
    return pl.pallas_call(
        merge_kernel,
        out_shape=(jax.ShapeDtypeStruct((ROWS, BLOCK), F32), piece, piece),
        in_specs=[SMEM, VMEM, VMEM],
        out_specs=(VMEM, VMEM, VMEM),
        compiler_params=PARAMS,
        name="merge",
    )(place, mine, theirs)


def short(proj, taps):
    n = proj.shape[0] - HALO
    return (
        taps[0:1] * proj[HALO : HALO + n]
        + taps[1:2] * proj[HALO - 1 : HALO - 1 + n]
        + taps[2:3] * proj[HALO - 2 : HALO - 2 + n]
    )


def drive_kernel(place, mine, theirs, taps, weigh, step, driven, before, state, signal, total):
    spot = place[0] & 3
    core = place[0] & 1
    first = jnp.where(core == 0, taps[1], taps[2])
    second = jnp.where(core == 0, taps[2], taps[1])
    signal[...] = short(mine[...].astype(F32), first) * short(theirs[...].astype(F32), second)
    start = pl.multiple_of(spot * BLOCK, BLOCK)
    driven[...] = signal[pl.ds(start, BLOCK)]
    for r in range(MODES):
        w, decay = weigh[r], step[r : r + 1]
        past = jnp.zeros((1, BLOCK), F32)
        held = past
        for b in range(4):
            held = jnp.where(spot == b, past, held)
            past = decay * past + jnp.sum(w * signal[BLOCK * b : BLOCK * b + BLOCK], axis=0, keepdims=True)
        before[r : r + 1] = held
        total[r : r + 1] = past
    for i in range(16):
        state[i] = total[...]


def drive(place, mine, theirs, taps, weigh, step):
    square = jax.ShapeDtypeStruct((BLOCK, BLOCK), F32)
    modes = jax.ShapeDtypeStruct((MODES, BLOCK), F32)
    copies = jax.ShapeDtypeStruct((16, MODES, BLOCK), F32)
    return pl.pallas_call(
        drive_kernel,
        out_shape=(square, modes, copies),
        in_specs=[SMEM] + [VMEM] * 5,
        out_specs=(VMEM,) * 3,
        scratch_shapes=[pltpu.VMEM((GROUP, BLOCK), F32), pltpu.VMEM((MODES, BLOCK), F32)],
        compiler_params=PARAMS,
        name="drive",
    )(place, mine, theirs, taps, weigh, step)


def tables_kernel(place, residues, rates, weigh, reach, taps, step, last):
    at = place[0]
    index = lax.broadcasted_iota(jnp.int32, (BLOCK, BLOCK), 0).astype(F32)
    total = jnp.zeros((BLOCK, BLOCK), F32)
    for r in range(MODES):
        rate = rates[r : r + 1]
        amount = residues[r : r + 1] * jnp.sqrt(2.0 * rate)
        weigh[r] = jnp.exp(-rate * (BLOCK - 1.0 - index))
        reach[r] = amount * jnp.exp(-rate * (index + 1.0))
        total = total + amount * jnp.exp(-rate * index)
    taps[...] = total
    rate = rates[...]
    step[...] = jnp.exp(-rate * float(BLOCK))
    for i in range(16):
        after = at - 4 * (i + 1)
        decay = jnp.exp(-rate * (BLOCK * jnp.maximum(after, 0)).astype(F32))
        last[i] = jnp.where(after >= 0, decay, 0.0)


def tables(place, residues, rates):
    def full(*shape):
        return jax.ShapeDtypeStruct(shape, F32)

    return pl.pallas_call(
        tables_kernel,
        out_shape=(
            full(MODES, BLOCK, BLOCK),
            full(MODES, BLOCK, BLOCK),
            full(BLOCK, BLOCK),
            full(MODES, BLOCK),
            full(16, MODES, BLOCK),
        ),
        in_specs=[SMEM, VMEM, VMEM],
        out_specs=(VMEM,) * 5,
        compiler_params=PARAMS,
        name="tables",
    )(place, residues, rates)


def near_kernel(driven, taps, gain, out, padded):
    signal = driven[...]
    padded[:BLOCK] = jnp.zeros((BLOCK, BLOCK), F32)
    padded[BLOCK:] = signal
    total = gain[...] * signal
    for s in range(BLOCK):
        low = s // 8 * 8
        part = taps[s : s + 1] * padded[BLOCK + low - s : 2 * BLOCK - s]
        if low:
            part = jnp.concatenate([jnp.zeros((low, BLOCK), F32), part], axis=0)
        total = total + part
    out[...] = total


def near(driven, taps, gain):
    return pl.pallas_call(
        near_kernel,
        out_shape=jax.ShapeDtypeStruct((BLOCK, BLOCK), F32),
        in_specs=[VMEM] * 3,
        out_specs=VMEM,
        scratch_shapes=[pltpu.VMEM((2 * BLOCK, BLOCK), F32)],
        compiler_params=PARAMS,
        cost_estimate=pl.CostEstimate(flops=2 * BLOCK**3, bytes_accessed=3 * BLOCK * BLOCK * 4, transcendentals=0),
        name="near",
    )(driven, taps, gain)


def finish_kernel(own, other, taps, inner, reach, before, states, last, out):
    query = short((own[...] + other[...]).astype(BF16).astype(F32), taps[0])
    carry = before[...]
    for i in range(16):
        carry = carry + last[i] * states[i]
    conv = inner[...]
    for r in range(MODES):
        conv = conv + reach[r] * carry[r : r + 1]
    out[...] = (query * conv).T


def finish(own, other, taps, inner, reach, before, states, last):
    return pl.pallas_call(
        finish_kernel,
        out_shape=jax.ShapeDtypeStruct((BLOCK, BLOCK), F32),
        in_specs=[VMEM] * 8,
        out_specs=VMEM,
        compiler_params=PARAMS,
        name="finish",
    )(own, other, taps, inner, reach, before, states, last)


def body(tokens, in_weight, short_taps, residues, rates, skip_gain):
    place = lax.axis_index("ctx")
    tp = lax.axis_index("tp")
    spot = place[None]
    apart = tp ^ (place >> 3)
    match = jnp.stack([apart >> 1, apart & 1, place & 1, tp & 3])

    near_h, far_h, weights = gather(tokens, in_weight, place)
    weigh, reach, taps, step, last = tables(spot, residues.T, rates.T)

    mine, gift = project(match, near_h, far_h, weights)
    pair, own, gift = merge(spot, mine, flip(gift, "ctx", 1))
    mine = (pair + flip(pair, "ctx", 2)).astype(BF16)
    other = flip(gift, "ctx", 2)
    short_rows = short_taps.transpose(0, 2, 1)
    driven, before, state = drive(spot, mine, flip(mine, "ctx", 1), short_rows, weigh, step)
    inner = near(driven, taps, skip_gain[None])
    return finish(own, other, short_rows, inner, reach, before, swap(state, "ctx", GROUPS), last)


def solution(mesh):
    in_specs = (
        P("ctx", "tp"),
        P(None, "ctx", "tp"),
        P(None, "tp", None),
        P("tp", None),
        P("tp", None),
        P("tp"),
    )
    return jax.shard_map(
        body, mesh=mesh, in_specs=in_specs, out_specs=P("tp", "ctx"), check_vma=False
    )
```

```python
import jax
import jax.numpy as jnp
from jax import lax
from jax.experimental import pallas as pl
from jax.experimental.pallas import tpu as pltpu
from jax.sharding import PartitionSpec as P

F32 = jnp.float32
BF16 = jnp.bfloat16
HALO = 16
BLOCK = 128
GROUP = 4 * BLOCK
ROWS = HALO + GROUP
PIECE = HALO + BLOCK
OWN = 2 * PIECE
MODES = 16
VMEM = pl.BlockSpec(memory_space=pltpu.VMEM)
SMEM = pl.BlockSpec(memory_space=pltpu.SMEM)
PARAMS = pltpu.CompilerParams(vmem_limit_bytes=48 * 1024 * 1024)


def flip(x, axis, mask):
    length = lax.axis_size(axis)
    return lax.ppermute(x, axis, [(i, i ^ mask) for i in range(length)])


def ahead(x, axis, by):
    length = lax.axis_size(axis)
    return lax.ppermute(x, axis, [(i, i + by) for i in range(length - by)])


def ordered(upper, own, other, axis):
    first = jnp.where(upper, other, own)
    second = jnp.where(upper, own, other)
    return jnp.concatenate([first, second], axis=axis)


def share(x, axis, groups):
    size = len(groups[0])
    return swap(jnp.broadcast_to(x[None], (size,) + x.shape), axis, groups)


def swap(x, axis, groups):
    return lax.all_to_all(x, axis, 0, 0, axis_index_groups=groups)


NEIGHBOURS = [[4 * i + j for j in range(4)] for i in range(16)]
GROUPS = [[4 * i + low for i in range(16)] for low in range(4)]
ROUND = [[0, 1, 2, 3], [4, 5, 6, 7]]


def flip_many(x, axis, masks):
    return [flip(x, axis, m) for m in masks]


def split_kernel(place, tokens, kept, given):
    core = place[0] & 1
    for out, side in ((kept, core), (given, 1 - core)):
        for bit8 in range(2):
            for bit9 in range(2):
                start = pl.multiple_of(512 * bit9 + 256 * bit8 + side * 128, 128)
                out[bit8, :, 128 * bit9 : 128 * bit9 + 128] = tokens[:, pl.ds(start, 128)]


def insert_kernel(place, kept_rows, given_rows, halo, kept, given):
    core = place[0] & 1
    for out, rows, side in ((kept, kept_rows, core), (given, given_rows, 1 - core)):
        out[:, HALO:] = rows[...]
        for bit8 in range(2):
            for bit9 in range(2):
                start = pl.multiple_of(512 * bit9 + 256 * bit8 + side * 128, 128)
                out[bit8, :HALO, 128 * bit9 : 128 * bit9 + 128] = halo[:, pl.ds(start, 128)]


def split(place, tokens, halo):
    def call(kernel, rows, name, *args):
        shape = jax.ShapeDtypeStruct((2, rows, 256), BF16)
        return pl.pallas_call(
            kernel,
            out_shape=(shape, shape),
            in_specs=[SMEM] + [VMEM] * len(args),
            out_specs=(VMEM, VMEM),
            compiler_params=PARAMS,
            name=name,
        )(place, *args)

    return call(insert_kernel, PIECE, "insert", *call(split_kernel, BLOCK, "split", tokens), halo)


def joined(upper, own, other, axis):
    first = jnp.where(upper, other, own)
    second = jnp.where(upper, own, other)
    rest = lax.slice_in_dim(second, HALO, second.shape[axis], axis=axis)
    return jnp.concatenate([first, rest], axis=axis)


def gather(tokens, in_weight, place):
    held = jnp.concatenate([in_weight[1], in_weight[2], in_weight[0]], axis=1)[None]
    held = jnp.concatenate([held, flip(held, "ctx", 8)], axis=0)
    held = ordered((place & 4) == 4, held, flip(held, "ctx", 4), 1)
    weights = [held] + flip_many(held, "ctx", (16, 32, 48))
    halo = ahead(tokens[BLOCK - HALO :], "ctx", 1)
    kept, given = split(place[None], tokens, halo)
    both = joined((place & 1) == 1, kept, flip(given, "ctx", 1), 1)
    upper = (place & 2) == 2
    keep = jnp.where(upper, both[1], both[0])
    give = jnp.where(upper, both[0], both[1])
    near_h = joined(upper, keep, flip(give, "ctx", 2), 0)
    turns = [near_h] + flip_many(near_h, "tp", (1, 2, 3))
    far_h, turns[:3] = lax.optimization_barrier((flip(near_h, "tp", 4), turns[:3]))
    return turns, share(far_h, "tp", ROUND), weights


def project_kernel(match, t0, t1, t2, t3, far_ref, w0, w1, w2, w3, kept, given, total, far_h, t3_here, landed):
    bring = pltpu.make_async_copy(far_ref, far_h, landed.at[0])
    bring.start()
    also = pltpu.make_async_copy(t3, t3_here, landed.at[1])
    also.start()
    near_h, weights = (t0, t1, t2, t3_here), (w0, w1, w2, w3)

    def some(case, turn_h, turns):
        added = jnp.zeros(total.shape, F32)
        for turn_y in turns:
            part = far_h[match[3] ^ turn_y] if turn_h else near_h[turn_y][...]
            turn_x = case ^ (turn_h << 1 | turn_y >> 1)
            weight = weights[turn_x][match[1] ^ (turn_y & 1)]
            added += jnp.dot(part, weight, preferred_element_type=F32)
        return added

    for case in range(4):

        @pl.when(match[0] == case)
        def _():
            total[...] = some(case, 0, (0, 1, 2))

    also.wait()
    bring.wait()
    for case in range(4):

        @pl.when(match[0] == case)
        def _():
            total[...] += some(case, 0, (3,)) + some(case, 1, (0, 1, 2, 3))

    for core in range(2):

        @pl.when(match[2] == core)
        def _():
            for out, side in ((kept, core), (given, 1 - core)):
                out[:ROWS] = total[:, BLOCK * side : BLOCK * side + BLOCK]
                for chip in range(2):
                    start = BLOCK * (2 * chip + side)
                    out[ROWS + PIECE * chip : ROWS + PIECE * chip + PIECE] = total[
                        start : start + PIECE, 2 * BLOCK :
                    ]


def project(match, near_h, far_h, weights):
    columns = weights[0].shape[2]
    shape = jax.ShapeDtypeStruct((ROWS + OWN, BLOCK), F32)
    return pl.pallas_call(
        project_kernel,
        out_shape=(shape, shape),
        in_specs=[SMEM] + [VMEM] * 3 + [pl.BlockSpec(memory_space=pl.ANY)] * 2 + [VMEM] * 4,
        out_specs=(VMEM, VMEM),
        scratch_shapes=[
            pltpu.VMEM((ROWS, columns), F32),
            pltpu.VMEM(far_h.shape, BF16),
            pltpu.VMEM(far_h.shape[1:], BF16),
            pltpu.SemaphoreType.DMA((2,)),
        ],
        compiler_params=PARAMS,
        cost_estimate=pl.CostEstimate(
            flops=2 * ROWS * 2048 * columns, bytes_accessed=2048 * 2 * (ROWS + columns), transcendentals=0
        ),
        name="project",
    )(match, *near_h, far_h, *weights)


def merge_kernel(place, mine, theirs, pair, query, gift):
    pair[...] = mine[:ROWS] + theirs[:ROWS]
    chip = (place[0] >> 1) & 1
    for out, side in ((query, chip), (gift, 1 - chip)):
        start = pl.multiple_of(ROWS + PIECE * side, 16)
        out[...] = mine[pl.ds(start, PIECE)] + theirs[pl.ds(start, PIECE)]


def merge(place, mine, theirs):
    piece = jax.ShapeDtypeStruct((PIECE, BLOCK), F32)
    return pl.pallas_call(
        merge_kernel,
        out_shape=(jax.ShapeDtypeStruct((ROWS, BLOCK), F32), piece, piece),
        in_specs=[SMEM, VMEM, VMEM],
        out_specs=(VMEM, VMEM, VMEM),
        compiler_params=PARAMS,
        name="merge",
    )(place, mine, theirs)


def short(proj, taps):
    n = proj.shape[0] - HALO
    return (
        taps[0:1] * proj[HALO : HALO + n]
        + taps[1:2] * proj[HALO - 1 : HALO - 1 + n]
        + taps[2:3] * proj[HALO - 2 : HALO - 2 + n]
    )


def drive_kernel(place, mine, theirs, taps, weigh, step, driven, before, state, signal, total):
    spot = place[0] & 3
    core = place[0] & 1
    first = jnp.where(core == 0, taps[1], taps[2])
    second = jnp.where(core == 0, taps[2], taps[1])
    signal[...] = short(mine[...].astype(F32), first) * short(theirs[...].astype(F32), second)
    start = pl.multiple_of(spot * BLOCK, BLOCK)
    driven[...] = signal[pl.ds(start, BLOCK)]
    for r in range(MODES):
        w, decay = weigh[r], step[r : r + 1]
        past = jnp.zeros((1, BLOCK), F32)
        held = past
        for b in range(4):
            held = jnp.where(spot == b, past, held)
            past = decay * past + jnp.sum(w * signal[BLOCK * b : BLOCK * b + BLOCK], axis=0, keepdims=True)
        before[r : r + 1] = held
        total[r : r + 1] = past
    for i in range(16):
        state[i] = total[...]


def drive(place, mine, theirs, taps, weigh, step):
    square = jax.ShapeDtypeStruct((BLOCK, BLOCK), F32)
    modes = jax.ShapeDtypeStruct((MODES, BLOCK), F32)
    copies = jax.ShapeDtypeStruct((16, MODES, BLOCK), F32)
    return pl.pallas_call(
        drive_kernel,
        out_shape=(square, modes, copies),
        in_specs=[SMEM] + [VMEM] * 5,
        out_specs=(VMEM,) * 3,
        scratch_shapes=[pltpu.VMEM((GROUP, BLOCK), F32), pltpu.VMEM((MODES, BLOCK), F32)],
        compiler_params=PARAMS,
        name="drive",
    )(place, mine, theirs, taps, weigh, step)


def tables_kernel(place, residues, rates, weigh, reach, taps, step, last):
    at = place[0]
    index = lax.broadcasted_iota(jnp.int32, (BLOCK, BLOCK), 0).astype(F32)
    total = jnp.zeros((BLOCK, BLOCK), F32)
    for r in range(MODES):
        rate = rates[r : r + 1]
        amount = residues[r : r + 1] * jnp.sqrt(2.0 * rate)
        weigh[r] = jnp.exp(-rate * (BLOCK - 1.0 - index))
        reach[r] = amount * jnp.exp(-rate * (index + 1.0))
        total = total + amount * jnp.exp(-rate * index)
    taps[...] = total
    rate = rates[...]
    step[...] = jnp.exp(-rate * float(BLOCK))
    for i in range(16):
        after = at - 4 * (i + 1)
        decay = jnp.exp(-rate * (BLOCK * jnp.maximum(after, 0)).astype(F32))
        last[i] = jnp.where(after >= 0, decay, 0.0)


def tables(place, residues, rates):
    def full(*shape):
        return jax.ShapeDtypeStruct(shape, F32)

    return pl.pallas_call(
        tables_kernel,
        out_shape=(
            full(MODES, BLOCK, BLOCK),
            full(MODES, BLOCK, BLOCK),
            full(BLOCK, BLOCK),
            full(MODES, BLOCK),
            full(16, MODES, BLOCK),
        ),
        in_specs=[SMEM, VMEM, VMEM],
        out_specs=(VMEM,) * 5,
        compiler_params=PARAMS,
        name="tables",
    )(place, residues, rates)


def near_kernel(driven, taps, gain, out, padded):
    signal = driven[...]
    padded[:BLOCK] = jnp.zeros((BLOCK, BLOCK), F32)
    padded[BLOCK:] = signal
    total = gain[...] * signal
    for s in range(BLOCK):
        low = s // 8 * 8
        part = taps[s : s + 1] * padded[BLOCK + low - s : 2 * BLOCK - s]
        if low:
            part = jnp.concatenate([jnp.zeros((low, BLOCK), F32), part], axis=0)
        total = total + part
    out[...] = total


def near(driven, taps, gain):
    return pl.pallas_call(
        near_kernel,
        out_shape=jax.ShapeDtypeStruct((BLOCK, BLOCK), F32),
        in_specs=[VMEM] * 3,
        out_specs=VMEM,
        scratch_shapes=[pltpu.VMEM((2 * BLOCK, BLOCK), F32)],
        compiler_params=PARAMS,
        cost_estimate=pl.CostEstimate(flops=2 * BLOCK**3, bytes_accessed=3 * BLOCK * BLOCK * 4, transcendentals=0),
        name="near",
    )(driven, taps, gain)


def finish_kernel(own, other, taps, inner, reach, before, states, last, out):
    query = short((own[...] + other[...]).astype(BF16).astype(F32), taps[0])
    carry = before[...]
    for i in range(16):
        carry = carry + last[i] * states[i]
    conv = inner[...]
    for r in range(MODES):
        conv = conv + reach[r] * carry[r : r + 1]
    out[...] = (query * conv).T


def finish(own, other, taps, inner, reach, before, states, last):
    return pl.pallas_call(
        finish_kernel,
        out_shape=jax.ShapeDtypeStruct((BLOCK, BLOCK), F32),
        in_specs=[VMEM] * 8,
        out_specs=VMEM,
        compiler_params=PARAMS,
        name="finish",
    )(own, other, taps, inner, reach, before, states, last)


def body(tokens, in_weight, short_taps, residues, rates, skip_gain):
    place = lax.axis_index("ctx")
    tp = lax.axis_index("tp")
    spot = place[None]
    apart = tp ^ (place >> 3)
    match = jnp.stack([apart >> 1, apart & 1, place & 1, tp & 3])

    near_h, far_h, weights = gather(tokens, in_weight, place)
    weigh, reach, taps, step, last = tables(spot, residues.T, rates.T)

    mine, gift = project(match, near_h, far_h, weights)
    pair, own, gift = merge(spot, mine, flip(gift, "ctx", 1))
    mine = (pair + flip(pair, "ctx", 2)).astype(BF16)
    other = flip(gift, "ctx", 2)
    short_rows = short_taps.transpose(0, 2, 1)
    driven, before, state = drive(spot, mine, flip(mine, "ctx", 1), short_rows, weigh, step)
    inner = near(driven, taps, skip_gain[None])
    return finish(own, other, short_rows, inner, reach, before, swap(state, "ctx", GROUPS), last)


def solution(mesh):
    in_specs = (
        P("ctx", "tp"),
        P(None, "ctx", "tp"),
        P(None, "tp", None),
        P("tp", None),
        P("tp", None),
        P("tp"),
    )
    return jax.shard_map(
        body, mesh=mesh, in_specs=in_specs, out_specs=P("tp", "ctx"), check_vma=False
    )
```

```python
import jax
import jax.numpy as jnp
from jax import lax
from jax.experimental import pallas as pl
from jax.experimental.pallas import tpu as pltpu
from jax.sharding import PartitionSpec as P

F32 = jnp.float32
BF16 = jnp.bfloat16
HALO = 16
BLOCK = 128
GROUP = 4 * BLOCK
ROWS = HALO + GROUP
PIECE = HALO + BLOCK
OWN = 2 * PIECE
MODES = 16
VMEM = pl.BlockSpec(memory_space=pltpu.VMEM)
SMEM = pl.BlockSpec(memory_space=pltpu.SMEM)
PARAMS = pltpu.CompilerParams(vmem_limit_bytes=48 * 1024 * 1024)


def flip(x, axis, mask):
    length = lax.axis_size(axis)
    return lax.ppermute(x, axis, [(i, i ^ mask) for i in range(length)])


def ahead(x, axis, by):
    length = lax.axis_size(axis)
    return lax.ppermute(x, axis, [(i, i + by) for i in range(length - by)])


def ordered(upper, own, other, axis):
    first = jnp.where(upper, other, own)
    second = jnp.where(upper, own, other)
    return jnp.concatenate([first, second], axis=axis)


def share(x, axis, groups):
    size = len(groups[0])
    return swap(jnp.broadcast_to(x[None], (size,) + x.shape), axis, groups)


def swap(x, axis, groups):
    return lax.all_to_all(x, axis, 0, 0, axis_index_groups=groups)


NEIGHBOURS = [[4 * i + j for j in range(4)] for i in range(16)]
GROUPS = [[4 * i + low for i in range(16)] for low in range(4)]
ROUND = [[0, 1, 2, 3], [4, 5, 6, 7]]


def flip_many(x, axis, masks):
    return [flip(x, axis, m) for m in masks]


def split_kernel(place, tokens, kept, given):
    core = place[0] & 1
    for out, side in ((kept, core), (given, 1 - core)):
        for bit8 in range(2):
            for bit9 in range(2):
                start = pl.multiple_of(512 * bit9 + 256 * bit8 + side * 128, 128)
                out[bit8, :, 128 * bit9 : 128 * bit9 + 128] = tokens[:, pl.ds(start, 128)]


def insert_kernel(place, kept_rows, given_rows, halo, kept, given):
    core = place[0] & 1
    for out, rows, side in ((kept, kept_rows, core), (given, given_rows, 1 - core)):
        out[:, HALO:] = rows[...]
        for bit8 in range(2):
            for bit9 in range(2):
                start = pl.multiple_of(512 * bit9 + 256 * bit8 + side * 128, 128)
                out[bit8, :HALO, 128 * bit9 : 128 * bit9 + 128] = halo[:, pl.ds(start, 128)]


def split(place, tokens, halo):
    def call(kernel, rows, name, *args):
        shape = jax.ShapeDtypeStruct((2, rows, 256), BF16)
        return pl.pallas_call(
            kernel,
            out_shape=(shape, shape),
            in_specs=[SMEM] + [VMEM] * len(args),
            out_specs=(VMEM, VMEM),
            compiler_params=PARAMS,
            name=name,
        )(place, *args)

    return call(insert_kernel, PIECE, "insert", *call(split_kernel, BLOCK, "split", tokens), halo)


def joined(upper, own, other, axis):
    first = jnp.where(upper, other, own)
    second = jnp.where(upper, own, other)
    rest = lax.slice_in_dim(second, HALO, second.shape[axis], axis=axis)
    return jnp.concatenate([first, rest], axis=axis)


def gather(tokens, in_weight, place):
    held = jnp.concatenate([in_weight[1], in_weight[2], in_weight[0]], axis=1)[None]
    held = jnp.concatenate([held, flip(held, "ctx", 8)], axis=0)
    held = ordered((place & 4) == 4, held, flip(held, "ctx", 4), 1)
    weights = [held] + flip_many(held, "ctx", (16, 32, 48))
    halo = ahead(tokens[BLOCK - HALO :], "ctx", 1)
    kept, given = split(place[None], tokens, halo)
    both = joined((place & 1) == 1, kept, flip(given, "ctx", 1), 1)
    upper = (place & 2) == 2
    keep = jnp.where(upper, both[1], both[0])
    give = jnp.where(upper, both[0], both[1])
    near_h = joined(upper, keep, flip(give, "ctx", 2), 0)
    turns = [near_h] + flip_many(near_h, "tp", (1, 2, 3))
    far_h, turns[:3] = lax.optimization_barrier((flip(near_h, "tp", 4), turns[:3]))
    return turns, share(far_h, "tp", ROUND), weights


def project_kernel(match, t0, t1, t2, t3, far_ref, w0, w1, w2, w3, kept, given, total, far_h, t3_here, landed):
    also = pltpu.make_async_copy(t3, t3_here, landed.at[4])
    also.start()
    bring = [pltpu.make_async_copy(far_ref.at[match[3] ^ i], far_h.at[i], landed.at[i]) for i in range(4)]
    for copy in bring:
        copy.start()
    near_h, weights = (t0, t1, t2, t3_here), (w0, w1, w2, w3)

    def some(case, turn_h, turns):
        added = jnp.zeros(total.shape, F32)
        for turn_y in turns:
            part = far_h[turn_y] if turn_h else near_h[turn_y][...]
            turn_x = case ^ (turn_h << 1 | turn_y >> 1)
            weight = weights[turn_x][match[1] ^ (turn_y & 1)]
            added += jnp.dot(part, weight, preferred_element_type=F32)
        return added

    for case in range(4):

        @pl.when(match[0] == case)
        def _():
            total[...] = some(case, 0, (0, 1, 2))

    also.wait()
    for step in range(2):
        for copy in bring[2 * step : 2 * step + 2]:
            copy.wait()
        for case in range(4):

            @pl.when(match[0] == case)
            def _():
                added = some(case, 1, (2 * step, 2 * step + 1))
                total[...] += added if step else added + some(case, 0, (3,))

    for core in range(2):

        @pl.when(match[2] == core)
        def _():
            for out, side in ((kept, core), (given, 1 - core)):
                out[:ROWS] = total[:, BLOCK * side : BLOCK * side + BLOCK]
                for chip in range(2):
                    start = BLOCK * (2 * chip + side)
                    out[ROWS + PIECE * chip : ROWS + PIECE * chip + PIECE] = total[
                        start : start + PIECE, 2 * BLOCK :
                    ]


def project(match, near_h, far_h, weights):
    columns = weights[0].shape[2]
    shape = jax.ShapeDtypeStruct((ROWS + OWN, BLOCK), F32)
    return pl.pallas_call(
        project_kernel,
        out_shape=(shape, shape),
        in_specs=[SMEM] + [VMEM] * 3 + [pl.BlockSpec(memory_space=pl.ANY)] * 2 + [VMEM] * 4,
        out_specs=(VMEM, VMEM),
        scratch_shapes=[
            pltpu.VMEM((ROWS, columns), F32),
            pltpu.VMEM(far_h.shape, BF16),
            pltpu.VMEM(far_h.shape[1:], BF16),
            pltpu.SemaphoreType.DMA((5,)),
        ],
        compiler_params=PARAMS,
        cost_estimate=pl.CostEstimate(
            flops=2 * ROWS * 2048 * columns, bytes_accessed=2048 * 2 * (ROWS + columns), transcendentals=0
        ),
        name="project",
    )(match, *near_h, far_h, *weights)


def merge_kernel(place, mine, theirs, pair, query, gift):
    pair[...] = mine[:ROWS] + theirs[:ROWS]
    chip = (place[0] >> 1) & 1
    for out, side in ((query, chip), (gift, 1 - chip)):
        start = pl.multiple_of(ROWS + PIECE * side, 16)
        out[...] = mine[pl.ds(start, PIECE)] + theirs[pl.ds(start, PIECE)]


def merge(place, mine, theirs):
    piece = jax.ShapeDtypeStruct((PIECE, BLOCK), F32)
    return pl.pallas_call(
        merge_kernel,
        out_shape=(jax.ShapeDtypeStruct((ROWS, BLOCK), F32), piece, piece),
        in_specs=[SMEM, VMEM, VMEM],
        out_specs=(VMEM, VMEM, VMEM),
        compiler_params=PARAMS,
        name="merge",
    )(place, mine, theirs)


def short(proj, taps):
    n = proj.shape[0] - HALO
    return (
        taps[0:1] * proj[HALO : HALO + n]
        + taps[1:2] * proj[HALO - 1 : HALO - 1 + n]
        + taps[2:3] * proj[HALO - 2 : HALO - 2 + n]
    )


def drive_kernel(place, mine, theirs, taps, weigh, step, driven, before, state, signal, total):
    spot = place[0] & 3
    core = place[0] & 1
    first = jnp.where(core == 0, taps[1], taps[2])
    second = jnp.where(core == 0, taps[2], taps[1])
    signal[...] = short(mine[...].astype(F32), first) * short(theirs[...].astype(F32), second)
    start = pl.multiple_of(spot * BLOCK, BLOCK)
    driven[...] = signal[pl.ds(start, BLOCK)]
    for r in range(MODES):
        w, decay = weigh[r], step[r : r + 1]
        past = jnp.zeros((1, BLOCK), F32)
        held = past
        for b in range(4):
            held = jnp.where(spot == b, past, held)
            past = decay * past + jnp.sum(w * signal[BLOCK * b : BLOCK * b + BLOCK], axis=0, keepdims=True)
        before[r : r + 1] = held
        total[r : r + 1] = past
    for i in range(16):
        state[i] = total[...]


def drive(place, mine, theirs, taps, weigh, step):
    square = jax.ShapeDtypeStruct((BLOCK, BLOCK), F32)
    modes = jax.ShapeDtypeStruct((MODES, BLOCK), F32)
    copies = jax.ShapeDtypeStruct((16, MODES, BLOCK), F32)
    return pl.pallas_call(
        drive_kernel,
        out_shape=(square, modes, copies),
        in_specs=[SMEM] + [VMEM] * 5,
        out_specs=(VMEM,) * 3,
        scratch_shapes=[pltpu.VMEM((GROUP, BLOCK), F32), pltpu.VMEM((MODES, BLOCK), F32)],
        compiler_params=PARAMS,
        name="drive",
    )(place, mine, theirs, taps, weigh, step)


def tables_kernel(place, residues, rates, weigh, reach, taps, step, last):
    at = place[0]
    index = lax.broadcasted_iota(jnp.int32, (BLOCK, BLOCK), 0).astype(F32)
    total = jnp.zeros((BLOCK, BLOCK), F32)
    for r in range(MODES):
        rate = rates[r : r + 1]
        amount = residues[r : r + 1] * jnp.sqrt(2.0 * rate)
        weigh[r] = jnp.exp(-rate * (BLOCK - 1.0 - index))
        reach[r] = amount * jnp.exp(-rate * (index + 1.0))
        total = total + amount * jnp.exp(-rate * index)
    taps[...] = total
    rate = rates[...]
    step[...] = jnp.exp(-rate * float(BLOCK))
    for i in range(16):
        after = at - 4 * (i + 1)
        decay = jnp.exp(-rate * (BLOCK * jnp.maximum(after, 0)).astype(F32))
        last[i] = jnp.where(after >= 0, decay, 0.0)


def tables(place, residues, rates):
    def full(*shape):
        return jax.ShapeDtypeStruct(shape, F32)

    return pl.pallas_call(
        tables_kernel,
        out_shape=(
            full(MODES, BLOCK, BLOCK),
            full(MODES, BLOCK, BLOCK),
            full(BLOCK, BLOCK),
            full(MODES, BLOCK),
            full(16, MODES, BLOCK),
        ),
        in_specs=[SMEM, VMEM, VMEM],
        out_specs=(VMEM,) * 5,
        compiler_params=PARAMS,
        name="tables",
    )(place, residues, rates)


def near_kernel(driven, taps, gain, out, padded):
    signal = driven[...]
    padded[:BLOCK] = jnp.zeros((BLOCK, BLOCK), F32)
    padded[BLOCK:] = signal
    total = gain[...] * signal
    for s in range(BLOCK):
        low = s // 8 * 8
        part = taps[s : s + 1] * padded[BLOCK + low - s : 2 * BLOCK - s]
        if low:
            part = jnp.concatenate([jnp.zeros((low, BLOCK), F32), part], axis=0)
        total = total + part
    out[...] = total


def near(driven, taps, gain):
    return pl.pallas_call(
        near_kernel,
        out_shape=jax.ShapeDtypeStruct((BLOCK, BLOCK), F32),
        in_specs=[VMEM] * 3,
        out_specs=VMEM,
        scratch_shapes=[pltpu.VMEM((2 * BLOCK, BLOCK), F32)],
        compiler_params=PARAMS,
        cost_estimate=pl.CostEstimate(flops=2 * BLOCK**3, bytes_accessed=3 * BLOCK * BLOCK * 4, transcendentals=0),
        name="near",
    )(driven, taps, gain)


def finish_kernel(own, other, taps, inner, reach, before, states, last, out):
    query = short((own[...] + other[...]).astype(BF16).astype(F32), taps[0])
    carry = before[...]
    for i in range(16):
        carry = carry + last[i] * states[i]
    conv = inner[...]
    for r in range(MODES):
        conv = conv + reach[r] * carry[r : r + 1]
    out[...] = (query * conv).T


def finish(own, other, taps, inner, reach, before, states, last):
    return pl.pallas_call(
        finish_kernel,
        out_shape=jax.ShapeDtypeStruct((BLOCK, BLOCK), F32),
        in_specs=[VMEM] * 8,
        out_specs=VMEM,
        compiler_params=PARAMS,
        name="finish",
    )(own, other, taps, inner, reach, before, states, last)


def body(tokens, in_weight, short_taps, residues, rates, skip_gain):
    place = lax.axis_index("ctx")
    tp = lax.axis_index("tp")
    spot = place[None]
    apart = tp ^ (place >> 3)
    match = jnp.stack([apart >> 1, apart & 1, place & 1, tp & 3])

    near_h, far_h, weights = gather(tokens, in_weight, place)
    weigh, reach, taps, step, last = tables(spot, residues.T, rates.T)

    mine, gift = project(match, near_h, far_h, weights)
    pair, own, gift = merge(spot, mine, flip(gift, "ctx", 1))
    mine = (pair + flip(pair, "ctx", 2)).astype(BF16)
    other = flip(gift, "ctx", 2)
    short_rows = short_taps.transpose(0, 2, 1)
    driven, before, state = drive(spot, mine, flip(mine, "ctx", 1), short_rows, weigh, step)
    inner = near(driven, taps, skip_gain[None])
    return finish(own, other, short_rows, inner, reach, before, swap(state, "ctx", GROUPS), last)


def solution(mesh):
    in_specs = (
        P("ctx", "tp"),
        P(None, "ctx", "tp"),
        P(None, "tp", None),
        P("tp", None),
        P("tp", None),
        P("tp"),
    )
    return jax.shard_map(
        body, mesh=mesh, in_specs=in_specs, out_specs=P("tp", "ctx"), check_vma=False
    )
```
